32 devices in a mesh: grp: 2 (over y), blk: 4 (over z), bulk: 4 (over x, core).
Axes of the slice: x: 2, y: 2, z: 4, core: 2. Of those that a mesh axis runs over, the one named last changes fastest.
Arguments:
- tokens: bfloat16 [80, 8192], P(('grp', 'blk'), 'bulk'), parts along dimension 0, may hold values from -6 to 6
- cotangent: bfloat16 [80, 8192], P(('grp', 'blk'), 'bulk'), parts along dimension 0, may hold values from -1.5 to 1.5
- gate_weight: bfloat16 [8192, 26624], P('bulk', 'blk'), may hold values from -0.0625 to 0.0625
- up_weight: bfloat16 [8192, 26624], P('bulk', 'blk'), may hold values from -0.0625 to 0.0625
- down_weight: bfloat16 [26624, 8192], P('blk', 'bulk'), may hold values from -0.0390625 to 0.0390625
Outputs:
- mixed: bfloat16 [80, 8192], P(('grp', 'blk'), 'bulk'), parts along dimension 0
- grad_input: bfloat16 [80, 8192], P(('grp', 'blk'), 'bulk'), parts along dimension 0
The draws below stay inside these ranges and needn't reach their ends.
There are 2 independent parts, one for each index of `grp`. The reference program is written for one: setup_inputs(seed, part) draws one part's arguments, and reference() takes and returns one part's arrays. A program takes and returns all parts, laid end to end along the dimension named above; an argument that names none is the same for every part. Nothing has to cross between parts.
All inputs are finite; a program needn't handle non-finite values.
Results may differ from the reference program's by a relative error of at most 0.0049.
Values may be sent and summed in bfloat16 or wider, within the bound.
No kernel may reach another device: no remote copies, remote signals or barrier semaphores. Data moves between devices by JAX's collectives and lax.ppermute only.
A program may use at most 192 MiB of HBM per device.

```python
import jax
import jax.numpy as jnp
from jax import lax

D = 8192
FF = 26624
TOKENS = 40


def levels(rng, dims, split, low, largest):
    def one(position, shards_of):
        draws = jax.random.uniform(jax.random.fold_in(jax.random.fold_in(rng, 6), position), (shards_of,), jnp.float32, low / len(split), largest / len(split))
        return jnp.repeat(jnp.exp(draws), dims[position] // shards_of).reshape((-1,) + (1,) * (len(dims) - position - 1))

    loudness = one(*split[0])
    for cut in split[1:]:
        loudness = loudness * one(*cut)
    return loudness


def normal_values(stream_key, extent, scale, reach, cuts=(), dtype=jnp.bfloat16):
    gain = levels(stream_key, extent, cuts, -0.22, 0.18) if cuts else 1.0
    values = jax.random.normal(stream_key, extent, jnp.float32) * scale * gain
    return jnp.minimum(jnp.maximum(values, -reach), reach).astype(dtype)


def setup_inputs(seed: int = 0, part: int = 0) -> dict:
    seeds = jax.random.split(jax.random.key(seed), 6)
    own_keys = jax.random.split(jax.random.fold_in(seeds[5], part), 6)
    tokens = normal_values(own_keys[0], (TOKENS, D), 1.0, 6.0, ((0, 4), (1, 4)))
    cotangent = normal_values(own_keys[1], (TOKENS, D), 0.25, 1.5, ((0, 4), (1, 4)))
    gate_weight = normal_values(seeds[2], (D, FF), D ** -0.5, 0.0625, ((0, 4), (1, 4)))
    up_weight = normal_values(seeds[3], (D, FF), D ** -0.5, 0.0625, ((0, 4), (1, 4)))
    down_weight = normal_values(seeds[4], (FF, D), FF ** -0.5, 0.0390625, ((0, 4), (1, 4)))
    return {"tokens": tokens, "cotangent": cotangent, "gate_weight": gate_weight, "up_weight": up_weight, "down_weight": down_weight}


def reference(tokens, cotangent, gate_weight, up_weight, down_weight):
    gate = jnp.dot(tokens, gate_weight, preferred_element_type=jnp.float32)
    upward = jnp.dot(tokens, up_weight, preferred_element_type=jnp.float32)
    sigma = jax.nn.sigmoid(gate)
    hidden = (gate * sigma * upward).astype(jnp.bfloat16)
    mixed = jnp.dot(hidden, down_weight, preferred_element_type=jnp.float32).astype(jnp.bfloat16)
    back = lax.dot_general(cotangent, down_weight, (((1,), (1,)), ((), ())), preferred_element_type=jnp.float32)
    d_up = (back * gate * sigma).astype(jnp.bfloat16)
    d_gate = (back * upward * sigma * (1.0 + gate * (1.0 - sigma))).astype(jnp.bfloat16)
    first_part = lax.dot_general(d_gate, gate_weight, (((1,), (1,)), ((), ())), preferred_element_type=jnp.float32)
    second_part = lax.dot_general(d_up, up_weight, (((1,), (1,)), ((), ())), preferred_element_type=jnp.float32)
    grad_input = (first_part + second_part).astype(jnp.bfloat16)
    return mixed, grad_input
```

```python
import functools

import jax
import jax.numpy as jnp
from jax import lax
from jax.experimental import pallas as pl
from jax.experimental.pallas import tpu as pltpu
from jax.sharding import PartitionSpec as P

F32 = jnp.float32
BF16 = jnp.bfloat16
NT = (((1,), (1,)), ((), ()))
VMEM_LIMIT = 56 * 2**20


def swap(value, axis, size, bit):
    return lax.ppermute(value, axis, [(i, i ^ bit) for i in range(size)])


def bits(size, first=1):
    out = []
    while first < size:
        out.append(first)
        first *= 2
    return out


def tile(extent, largest):
    best = 128
    for t in range(128, largest + 1, 128):
        if extent % t == 0:
            best = t
    return best


def up_kernel(half, where, tok, cot, gate_w, up_w, down_w, keep, send, acc):
    step = pl.program_id(0)

    @pl.when(step == 0)
    def _():
        acc[...] = jnp.zeros_like(acc)

    acc[0] += jnp.dot(tok[...], gate_w[...], preferred_element_type=F32)
    acc[1] += jnp.dot(tok[...], up_w[...], preferred_element_type=F32)
    acc[2] += lax.dot_general(cot[...], down_w[...], NT, preferred_element_type=F32)

    @pl.when(step == pl.num_programs(0) - 1)
    def _():
        mine = pl.multiple_of(where[1] * half, 8)
        other = pl.multiple_of((1 - where[1]) * half, 8)
        keep[...] = acc[:, pl.ds(mine, half), :]
        send[...] = acc[:, pl.ds(other, half), :]


def up_call(where, tok, cot, gate_w, up_w, down_w, width, chunk, chunks):
    rows, feats = tok.shape
    half = rows // 2
    kt = tile(feats, 256)
    out = jax.ShapeDtypeStruct((3, half, width), F32)
    return pl.pallas_call(
        functools.partial(up_kernel, half),
        grid_spec=pltpu.PrefetchScalarGridSpec(
            num_scalar_prefetch=1,
            grid=(feats // kt,),
            in_specs=[
                pl.BlockSpec((rows, kt), lambda k, w: (0, k)),
                pl.BlockSpec((rows, kt), lambda k, w: (0, k)),
                pl.BlockSpec((kt, width), lambda k, w: (k, w[0] * chunks + chunk)),
                pl.BlockSpec((kt, width), lambda k, w: (k, w[0] * chunks + chunk)),
                pl.BlockSpec((width, kt), lambda k, w: (w[0] * chunks + chunk, k)),
            ],
            out_specs=[
                pl.BlockSpec((3, half, width), lambda k, w: (0, 0, 0)),
                pl.BlockSpec((3, half, width), lambda k, w: (0, 0, 0)),
            ],
            scratch_shapes=[pltpu.VMEM((3, rows, width), F32)],
        ),
        out_shape=[out, out],
        compiler_params=pltpu.CompilerParams(vmem_limit_bytes=VMEM_LIMIT),
        cost_estimate=pl.CostEstimate(
            flops=6 * rows * feats * width, bytes_accessed=6 * feats * width, transcendentals=0
        ),
        name="up",
    )(where, tok, cot, gate_w, up_w, down_w)


def down_kernel(half, padded, first, where, own, other, gate_w, up_w, down_w, *rest):
    if first:
        out, lhs = rest
    else:
        prev, out, lhs = rest

    @pl.when(pl.program_id(0) == 0)
    def _():
        lhs[:, :padded, :] = own[...]
        lhs[:, padded:, :] = other[...]

    mixed = jnp.dot(lhs[0], down_w[...], preferred_element_type=F32)
    grad = lax.dot_general(lhs[1], gate_w[...], NT, preferred_element_type=F32)
    grad += lax.dot_general(lhs[2], up_w[...], NT, preferred_element_type=F32)
    mine = pl.ds(pl.multiple_of(where[1] * half, 8), half)
    theirs = pl.ds(pl.multiple_of((1 - where[1]) * half, 8), half)
    for i, value in enumerate((mixed, grad)):
        a, b = value[:half], value[padded : padded + half]
        if not first:
            a, b = a + prev[i, mine, :], b + prev[i, theirs, :]
        out[i, mine, :] = a
        out[i, theirs, :] = b


def down_call(where, own, other, gate_w, up_w, down_w, prev, half, chunk, chunks):
    _, padded, width = own.shape
    feats = gate_w.shape[0]
    nt = tile(feats, 256)
    first = prev is None
    extra = [] if first else [pl.BlockSpec((2, 2 * half, nt), lambda j, w: (0, 0, j))]
    return pl.pallas_call(
        functools.partial(down_kernel, half, padded, first),
        grid_spec=pltpu.PrefetchScalarGridSpec(
            num_scalar_prefetch=1,
            grid=(feats // nt,),
            in_specs=[
                pl.BlockSpec((3, padded, width), lambda j, w: (0, 0, 0)),
                pl.BlockSpec((3, padded, width), lambda j, w: (0, 0, 0)),
                pl.BlockSpec((nt, width), lambda j, w: (j, w[0] * chunks + chunk)),
                pl.BlockSpec((nt, width), lambda j, w: (j, w[0] * chunks + chunk)),
                pl.BlockSpec((width, nt), lambda j, w: (w[0] * chunks + chunk, j)),
            ]
            + extra,
            out_specs=pl.BlockSpec((2, 2 * half, nt), lambda j, w: (0, 0, j)),
            scratch_shapes=[pltpu.VMEM((3, 2 * padded, width), BF16)],
        ),
        out_shape=jax.ShapeDtypeStruct((2, 2 * half, feats), F32),
        compiler_params=pltpu.CompilerParams(vmem_limit_bytes=VMEM_LIMIT),
        cost_estimate=pl.CostEstimate(
            flops=6 * 2 * half * feats * width, bytes_accessed=6 * feats * width, transcendentals=0
        ),
        name="down",
    )(where, own, other, gate_w, up_w, down_w, *([] if first else [prev]))


def per_device(sizes, tokens, cotangent, gate_weight, up_weight, down_weight):
    grp, blk, bulk = sizes["grp"], sizes["blk"], sizes["bulk"]
    units = gate_weight.shape[1]
    split = units % (grp * 128) == 0
    parts = grp if split else 1
    width = units // parts
    chunks = 2 if width % 256 == 0 else 1
    width //= chunks

    hops = [("blk", blk, b) for b in reversed(bits(blk))]
    if split:
        hops += [("grp", grp, b) for b in bits(grp)]
    tok, cot = tokens, cotangent
    for hop in hops:
        tok = jnp.concatenate([tok, swap(tok, *hop)], axis=0)
        cot = jnp.concatenate([cot, swap(cot, *hop)], axis=0)
    rows = tok.shape[0]
    half = rows // 2
    padded = -(-half // 16) * 16

    core = lax.axis_index("bulk") % 2
    group = lax.axis_index("grp") if split else jnp.int32(0)
    where = jnp.stack([group, core]).astype(jnp.int32)

    partial = [
        up_call(where, tok, cot, gate_weight, up_weight, down_weight, width, c, chunks)
        for c in range(chunks)
    ]
    total = None
    for c in range(chunks):
        keep, send = partial[c]
        sums = keep + swap(send, "bulk", bulk, 1)
        for b in bits(bulk, 2):
            sums = sums + swap(sums.astype(BF16), "bulk", bulk, b).astype(F32)
        gate, upward, back = sums[0], sums[1], sums[2]
        sigma = jax.nn.sigmoid(gate)
        hidden = gate * sigma * upward
        d_up = back * gate * sigma
        d_gate = back * upward * sigma * (1.0 + gate * (1.0 - sigma))
        own = jnp.stack([hidden, d_gate, d_up]).astype(BF16)
        own = jnp.pad(own, ((0, 0), (0, padded - half), (0, 0)))
        other = swap(own, "bulk", bulk, 1)
        total = down_call(
            where, own, other, gate_weight, up_weight, down_weight, total, half, c, chunks
        )

    for hop in reversed(hops):
        n = total.shape[1] // 2
        total = total[:, :n] + swap(total[:, n:].astype(BF16), *hop).astype(F32)
    total = total.astype(BF16)
    return total[0], total[1]


def solution(mesh):
    return jax.shard_map(
        functools.partial(per_device, dict(mesh.shape)),
        mesh=mesh,
        in_specs=(
            P(("grp", "blk"), "bulk"),
            P(("grp", "blk"), "bulk"),
            P("bulk", "blk"),
            P("bulk", "blk"),
            P("blk", "bulk"),
        ),
        out_specs=(P(("grp", "blk"), "bulk"), P(("grp", "blk"), "bulk")),
        check_vma=False,
    )
```

```python
import functools

import jax
import jax.numpy as jnp
from jax import lax
from jax.experimental import pallas as pl
from jax.experimental.pallas import tpu as pltpu
from jax.sharding import PartitionSpec as P

F32 = jnp.float32
BF16 = jnp.bfloat16
NT = (((1,), (1,)), ((), ()))
MIB = 2**20
VMEM = pl.BlockSpec(memory_space=pltpu.VMEM)
SMEM = pl.BlockSpec(memory_space=pltpu.SMEM)
HBM = pl.BlockSpec(memory_space=pltpu.HBM)
ANY = pl.BlockSpec(memory_space=pl.ANY)


def swap(value, axis, size, bit):
    return lax.ppermute(value, axis, [(i, i ^ bit) for i in range(size)])


def bits(size, first=1):
    out = []
    while first < size:
        out.append(first)
        first *= 2
    return out


def resident(x):
    return pltpu.with_memory_space_constraint(x, pltpu.VMEM)


def in_hbm(x):
    return pltpu.with_memory_space_constraint(x, pltpu.HBM)


def cost(flops, nbytes):
    return pl.CostEstimate(flops=flops, bytes_accessed=nbytes, transcendentals=0)


def call(kernel, name, in_specs, out_shape, scratch=(), limit=2, estimate=None):
    many = isinstance(out_shape, (list, tuple))
    return pl.pallas_call(
        kernel,
        in_specs=in_specs,
        out_specs=[VMEM] * len(out_shape) if many else VMEM,
        out_shape=out_shape,
        scratch_shapes=list(scratch),
        compiler_params=pltpu.CompilerParams(vmem_limit_bytes=limit * MIB),
        cost_estimate=estimate,
        name=name,
    )


def fetch(where, weight, dim, whole, start, size, after=()):
    shape = list(weight.shape)
    shape[dim] = size

    def kernel(where, src, *rest):
        out, sem = rest[-2:]
        first = pl.multiple_of(where[0] * whole + start, 128)
        part = src.at[pl.ds(first, size), :] if dim == 0 else src.at[:, pl.ds(first, size)]
        copy = pltpu.make_async_copy(part, out, sem)
        copy.start()
        copy.wait()

    return call(
        kernel,
        "fetch",
        [SMEM, HBM] + [ANY] * len(after),
        pltpu.VMEM(tuple(shape), BF16),
        [pltpu.SemaphoreType.DMA],
        estimate=cost(0, 2 * shape[0] * shape[1]),
    )(where, in_hbm(weight), *after)


def pack(tok_a, tok_b, cot_a, cot_b):
    n, feats = tok_a.shape

    def kernel(ta, tb, ca, cb, out, wide):
        for i, (a, b) in enumerate(((ta, tb), (ca, cb))):
            wide[i, :n, :] = a[...].astype(F32)
            wide[i, n : 2 * n, :] = b[...].astype(F32)
            out[i] = wide[i].astype(BF16)

    return call(
        kernel,
        "pack",
        [VMEM] * 4,
        jax.ShapeDtypeStruct((2, 2 * n, feats), BF16),
        [pltpu.VMEM((2, 2 * n, feats), F32)],
    )(tok_a, tok_b, cot_a, cot_b)


def repack(a, b):
    _, n, feats = a.shape

    def kernel(a, b, out, wide):
        for i in range(2):
            wide[i, :n, :] = a[i].astype(F32)
            wide[i, n : 2 * n, :] = b[i].astype(F32)
            out[i] = wide[i].astype(BF16)

    return call(
        kernel,
        "pack",
        [VMEM] * 2,
        jax.ShapeDtypeStruct((2, 2 * n, feats), BF16),
        [pltpu.VMEM((2, 2 * n, feats), F32)],
        limit=4,
    )(a, b)


def up(where, near, far, gate_w, up_w, down_w, block, after):
    _, half, feats = near.shape
    width = gate_w.shape[1]

    def kernel(where, near, far, gate_w, up_w, down_w, *rest):
        keep, send, wide, lhs = rest[-4:]
        first = where[1] == 0
        for i in range(2):
            a, b = near[i].astype(F32), far[i].astype(F32)
            wide[:half, :] = jnp.where(first, a, b)
            wide[half:, :] = jnp.where(first, b, a)
            lhs[i] = wide[...].astype(BF16)

        @pl.loop(0, width // block)
        def _(step):
            cut = pl.ds(pl.multiple_of(step * block, block), block)
            outs = (
                jnp.dot(lhs[0], gate_w[:, cut], preferred_element_type=F32),
                jnp.dot(lhs[0], up_w[:, cut], preferred_element_type=F32),
                lax.dot_general(lhs[1], down_w[cut, :], NT, preferred_element_type=F32),
            )
            for i, value in enumerate(outs):
                keep[i, :, cut] = value[:half]
                send[i, :, cut] = value[half:]

    out = jax.ShapeDtypeStruct((3, half, width), F32)
    return call(
        kernel,
        "up",
        [SMEM] + [VMEM] * 5 + [ANY] * len(after),
        [out, out],
        [pltpu.VMEM((2 * half, feats), F32), pltpu.VMEM((2, 2 * half, feats), BF16)],
        limit=8,
        estimate=cost(6 * 256 * feats * width, 6 * feats * width),
    )(where, near, far, resident(gate_w), resident(up_w), resident(down_w), *after)


def add(a, b):
    def kernel(a, b, total, rounded):
        value = a[...] + b[...].astype(F32)
        total[...] = value
        rounded[...] = value.astype(BF16)

    return call(
        kernel,
        "add",
        [VMEM] * 2,
        [jax.ShapeDtypeStruct(a.shape, F32), jax.ShapeDtypeStruct(a.shape, BF16)],
    )(a, b)


def activate(sums, got, padded):
    _, half, width = sums.shape

    def kernel(sums, got, out):
        gate = sums[0] + got[0].astype(F32)
        upward = sums[1] + got[1].astype(F32)
        back = sums[2] + got[2].astype(F32)
        sigma = jax.nn.sigmoid(gate)
        hidden = gate * sigma * upward
        d_up = back * gate * sigma
        d_gate = back * upward * sigma * (1.0 + gate * (1.0 - sigma))
        for i, value in enumerate((hidden, d_gate, d_up)):
            if padded > half:
                empty = jnp.zeros((padded - half, width), F32)
                value = jnp.concatenate([value, empty], axis=0)
            out[i] = value.astype(BF16)

    return call(
        kernel,
        "activate",
        [VMEM] * 2,
        jax.ShapeDtypeStruct((3, padded, width), BF16),
        limit=4,
    )(sums, got)


def down(where, own, other, gate_w, up_w, down_w, prev, half, which, last, block):
    _, padded, width = own.shape
    feats = down_w.shape[1] if down_w is not None else gate_w.shape[0]
    weights = ([down_w] if 0 in which else []) + ([gate_w, up_w] if 1 in which else [])
    used = ([0] if 0 in which else []) + ([1, 2] if 1 in which else [])

    def kernel(where, own, other, *rest):
        refs = list(rest)
        mixed_w = refs.pop(0) if 0 in which else None
        grad_w = (refs.pop(0), refs.pop(0)) if 1 in which else None
        before = [refs.pop(0) for _ in which] if prev else None
        lhs = refs.pop()
        first = where[1] == 0
        for i in used:
            lhs[i, :padded, :] = own[i]
            lhs[i, padded:, :] = other[i]

        @pl.loop(0, feats // block)
        def _(step):
            cut = pl.ds(pl.multiple_of(step * block, block), block)
            for n, i in enumerate(which):
                if i == 0:
                    value = jnp.dot(lhs[0], mixed_w[:, cut], preferred_element_type=F32)
                else:
                    value = lax.dot_general(
                        lhs[1], grad_w[0][cut, :], NT, preferred_element_type=F32
                    ) + lax.dot_general(lhs[2], grad_w[1][cut, :], NT, preferred_element_type=F32)
                if prev:
                    value += before[n][:, cut]
                if last:
                    a, b = value[:half], value[padded : padded + half]
                    refs[2 * n][:, cut] = jnp.where(first, a, b)
                    refs[2 * n + 1][:, cut] = jnp.where(first, b, a).astype(BF16)
                else:
                    refs[n][:, cut] = value

    if last:
        shapes = [
            jax.ShapeDtypeStruct((half, feats), F32),
            jax.ShapeDtypeStruct((half, feats), BF16),
        ] * len(which)
    else:
        shapes = [jax.ShapeDtypeStruct((2 * padded, feats), F32)] * len(which)
    return call(
        kernel,
        "down",
        [SMEM] + [VMEM] * (2 + len(weights) + len(which if prev else ())),
        shapes,
        [pltpu.VMEM((3, 2 * padded, width), BF16)],
        limit=8,
        estimate=cost(2 * len(used) * 256 * feats * width, 2 * len(used) * feats * width),
    )(where, own, other, *[resident(w) for w in weights], *(prev or ()))


def fold(keep, got):
    n, feats = keep.shape
    half = n // 2

    def kernel(keep, got, stay, send):
        value = keep[...] + got[...].astype(F32)
        stay[...] = value[:half]
        send[...] = value[half:].astype(BF16)

    return call(
        kernel,
        "fold",
        [VMEM] * 2,
        [jax.ShapeDtypeStruct((half, feats), F32), jax.ShapeDtypeStruct((half, feats), BF16)],
    )(keep, got)


def finish(keep, got):
    def kernel(keep, got, out):
        out[...] = (keep[...] + got[...].astype(F32)).astype(BF16)

    return call(kernel, "finish", [VMEM] * 2, jax.ShapeDtypeStruct(keep.shape, BF16))(keep, got)


def per_device(sizes, tokens, cotangent, gate_weight, up_weight, down_weight):
    grp, blk, bulk = sizes["grp"], sizes["blk"], sizes["bulk"]
    units, feats = gate_weight.shape[1], gate_weight.shape[0]
    split = units % (grp * 128) == 0
    whole = units // grp if split else units
    block = 256 if whole % 256 == 0 else 128
    blocks = whole // block
    cuts = [0, blocks // 2, blocks] if blocks > 1 else [0, blocks]
    chunks = [(a * block, (b - a) * block) for a, b in zip(cuts, cuts[1:])]
    down_block = 256 if feats % 256 == 0 else 128

    core = lax.axis_index("bulk") % 2
    group = lax.axis_index("grp") if split else jnp.int32(0)
    where = jnp.stack([group, core]).astype(jnp.int32)

    hops = [("blk", blk, b) for b in reversed(bits(blk))]
    if split:
        hops += [("grp", grp, b) for b in bits(grp)]
    near = pack(
        tokens, swap(tokens, *hops[0]), cotangent, swap(cotangent, *hops[0])
    )
    for hop in hops[1:-1]:
        near = repack(near, swap(near, *hop))
    far = swap(near, *hops[-1])
    half = near.shape[1]
    padded = -(-half // 16) * 16

    weights = [
        (
            fetch(where, gate_weight, 1, whole, start, size),
            fetch(where, up_weight, 1, whole, start, size),
            fetch(where, down_weight, 0, whole, start, size),
        )
        for start, size in chunks
    ]

    summed = []
    after = ()
    for w in weights:
        keep, send = up(where, near, far, *w, block, after)
        sums, rounded = add(keep, swap(send, "bulk", bulk, 1))
        after = (rounded,)
        summed.append((sums, rounded))

    prev = ()
    for c, (w, (sums, rounded)) in enumerate(zip(weights, summed)):
        for b in bits(bulk, 2)[:-1]:
            sums, rounded = add(sums, swap(rounded, "bulk", bulk, b))
        got = swap(rounded, "bulk", bulk, bits(bulk, 2)[-1])
        own = activate(sums, got, padded)
        other = swap(own, "bulk", bulk, 1)
        if c < len(chunks) - 1:
            prev = down(where, own, other, *w, prev, half, (0, 1), False, down_block)
    first = down(
        where, own, other, None, None, w[2], prev[:1], half, (0,), True, down_block
    )
    second = down(
        where, own, other, w[0], w[1], None, prev[1:], half, (1,), True, down_block
    )
    outs = []
    for stay, send in (first, second):
        for hop in reversed(hops[1:]):
            stay, send = fold(stay, swap(send, *hop))
        outs.append(finish(stay, swap(send, *hops[0])))
    return tuple(outs)


def solution(mesh):
    return jax.shard_map(
        functools.partial(per_device, dict(mesh.shape)),
        mesh=mesh,
        in_specs=(
            P(("grp", "blk"), "bulk"),
            P(("grp", "blk"), "bulk"),
            P("bulk", "blk"),
            P("bulk", "blk"),
            P("blk", "bulk"),
        ),
        out_specs=(P(("grp", "blk"), "bulk"), P(("grp", "blk"), "bulk")),
        check_vma=False,
    )
```

```python
import functools

import jax
import jax.numpy as jnp
from jax import lax
from jax.experimental import pallas as pl
from jax.experimental.pallas import tpu as pltpu
from jax.sharding import PartitionSpec as P

F32 = jnp.float32
BF16 = jnp.bfloat16
NT = (((1,), (1,)), ((), ()))
MIB = 2**20
VMEM = pl.BlockSpec(memory_space=pltpu.VMEM)
SMEM = pl.BlockSpec(memory_space=pltpu.SMEM)
HBM = pl.BlockSpec(memory_space=pltpu.HBM)
ANY = pl.BlockSpec(memory_space=pl.ANY)


def swap(value, axis, size, bit):
    return lax.ppermute(value, axis, [(i, i ^ bit) for i in range(size)])


def bits(size, first=1):
    out = []
    while first < size:
        out.append(first)
        first *= 2
    return out


def resident(x):
    return pltpu.with_memory_space_constraint(x, pltpu.VMEM)


def in_hbm(x):
    return pltpu.with_memory_space_constraint(x, pltpu.HBM)


def cost(flops, nbytes):
    return pl.CostEstimate(flops=flops, bytes_accessed=nbytes, transcendentals=0)


def call(kernel, name, in_specs, out_shape, scratch=(), limit=2, estimate=None):
    many = isinstance(out_shape, (list, tuple))
    return pl.pallas_call(
        kernel,
        in_specs=in_specs,
        out_specs=[VMEM] * len(out_shape) if many else VMEM,
        out_shape=out_shape,
        scratch_shapes=list(scratch),
        compiler_params=pltpu.CompilerParams(vmem_limit_bytes=limit * MIB),
        cost_estimate=estimate,
        name=name,
    )


def copies(where, specs, srcs, outs, sems):
    made = []
    for i, ((dim, whole, start, size), src, out) in enumerate(zip(specs, srcs, outs)):
        first = pl.multiple_of(where[0] * whole + start, 128)
        part = src.at[pl.ds(first, size), :] if dim == 0 else src.at[:, pl.ds(first, size)]
        made.append(pltpu.make_async_copy(part, out, sems.at[i]))
    return made


def fetched(weight, spec):
    shape = list(weight.shape)
    shape[spec[0]] = spec[3]
    return pltpu.VMEM(tuple(shape), BF16)


def fetch(where, wanted, after=()):
    weights, specs = zip(*wanted)
    n = len(wanted)

    def kernel(where, *refs):
        made = copies(where, specs, refs[:n], refs[n + len(after) : -1], refs[-1])
        for copy in made:
            copy.start()
        for copy in made:
            copy.wait()

    outs = [fetched(w, s) for w, s in wanted]
    return call(
        kernel,
        "fetch",
        [SMEM] + [HBM] * n + [ANY] * len(after),
        outs,
        [pltpu.SemaphoreType.DMA((n,))],
        estimate=cost(0, sum(2 * o.shape[0] * o.shape[1] for o in outs)),
    )(where, *[in_hbm(w) for w in weights], *after)


def pack(near, far, after):
    n, feats = near[0].shape[-2:]

    def kernel(*refs):
        out, wide = refs[-2:]
        for i in range(2):
            a, b = (refs[i], refs[2 + i]) if len(near) == 2 else (refs[0].at[i], refs[1].at[i])
            wide[i, :n, :] = a[...].astype(F32)
            wide[i, n : 2 * n, :] = b[...].astype(F32)
            out[i] = wide[i].astype(BF16)

    return call(
        kernel,
        "pack",
        [VMEM] * (len(near) + len(far)) + [ANY] * len(after),
        jax.ShapeDtypeStruct((2, 2 * n, feats), BF16),
        [pltpu.VMEM((2, 2 * n, feats), F32)],
        limit=4,
    )(*near, *far, *after)


def up(where, near, far, which, weights, transposed, block, wanted=(), after=()):
    _, half, feats = near.shape
    width = weights[0].shape[0 if transposed else 1]
    n, m = len(weights), len(wanted)
    specs = [s for _, s in wanted]

    def kernel(where, near, far, *refs):
        refs = list(refs)
        ws = [refs.pop(0) for _ in range(n)]
        srcs = [refs.pop(0) for _ in range(m)]
        del refs[: len(after)]
        outs = [refs.pop(0) for _ in range(2 * n)]
        dsts = [refs.pop(0) for _ in range(m)]
        wide, lhs = refs[:2]
        made = copies(where, specs, srcs, dsts, refs[2]) if m else []
        for copy in made:
            copy.start()
        first = where[1] == 0
        a, b = near[which].astype(F32), far[which].astype(F32)
        wide[:half, :] = jnp.where(first, a, b)
        wide[half:, :] = jnp.where(first, b, a)
        lhs[...] = wide[...].astype(BF16)

        @pl.loop(0, width // block)
        def _(step):
            cut = pl.ds(pl.multiple_of(step * block, block), block)
            for i, w in enumerate(ws):
                if transposed:
                    value = lax.dot_general(lhs[...], w[cut, :], NT, preferred_element_type=F32)
                else:
                    value = jnp.dot(lhs[...], w[:, cut], preferred_element_type=F32)
                outs[2 * i][:, cut] = value[:half]
                outs[2 * i + 1][:, cut] = value[half:]

        for copy in made:
            copy.wait()

    out = jax.ShapeDtypeStruct((half, width), F32)
    got = call(
        kernel,
        "up",
        [SMEM] + [VMEM] * (2 + n) + [HBM] * m + [ANY] * len(after),
        [out] * (2 * n) + [fetched(w, s) for w, s in wanted],
        [pltpu.VMEM((2 * half, feats), F32), pltpu.VMEM((2 * half, feats), BF16)]
        + ([pltpu.SemaphoreType.DMA((m,))] if m else []),
        limit=6,
        estimate=cost(2 * n * 256 * feats * width, 2 * n * feats * width),
    )(where, near, far, *[resident(w) for w in weights], *[in_hbm(w) for w, _ in wanted], *after)
    return got[: 2 * n : 2], got[1 : 2 * n : 2], got[2 * n :]


def gather(keeps, gots):
    n = len(keeps)
    shape = (n,) + keeps[0].shape

    def kernel(*refs):
        total, rounded = refs[-2:]
        for i in range(n):
            value = refs[i][...] + refs[n + i][...]
            total[i] = value
            rounded[i] = value.astype(BF16)

    return call(
        kernel,
        "gather",
        [VMEM] * (2 * n),
        [jax.ShapeDtypeStruct(shape, F32), jax.ShapeDtypeStruct(shape, BF16)],
    )(*keeps, *gots)


def add(a, b):
    def kernel(a, b, total, rounded):
        value = a[...] + b[...].astype(F32)
        total[...] = value
        rounded[...] = value.astype(BF16)

    return call(
        kernel,
        "add",
        [VMEM] * 2,
        [jax.ShapeDtypeStruct(a.shape, F32), jax.ShapeDtypeStruct(a.shape, BF16)],
    )(a, b)


def activate(sums, got, padded, after):
    _, half, width = sums.shape

    def kernel(sums, got, *rest):
        out = rest[-1]
        gate = sums[0] + got[0].astype(F32)
        upward = sums[1] + got[1].astype(F32)
        back = sums[2] + got[2].astype(F32)
        sigma = jax.nn.sigmoid(gate)
        hidden = gate * sigma * upward
        d_up = back * gate * sigma
        d_gate = back * upward * sigma * (1.0 + gate * (1.0 - sigma))
        for i, value in enumerate((hidden, d_gate, d_up)):
            if padded > half:
                empty = jnp.zeros((padded - half, width), F32)
                value = jnp.concatenate([value, empty], axis=0)
            out[i] = value.astype(BF16)

    return call(
        kernel,
        "activate",
        [VMEM] * 2 + [ANY] * len(after),
        jax.ShapeDtypeStruct((3, padded, width), BF16),
        limit=4,
    )(sums, got, *after)


def down(where, own, other, weights, prev, half, part, last, block):
    _, padded, width = own.shape
    start, feats = part

    def kernel(where, own, other, gate_w, up_w, down_w, *rest):
        lhs = rest[-1]
        outs = rest[len(prev) : -1]
        first = where[1] == 0
        lhs[:, :padded, :] = own[...]
        lhs[:, padded:, :] = other[...]

        @pl.loop(0, feats // block)
        def _(step):
            cut = pl.ds(pl.multiple_of(step * block, block), block)
            full = pl.ds(pl.multiple_of(start + step * block, block), block)
            mixed = jnp.dot(lhs[0], down_w[:, full], preferred_element_type=F32)
            grad = lax.dot_general(lhs[1], gate_w[full, :], NT, preferred_element_type=F32)
            grad += lax.dot_general(lhs[2], up_w[full, :], NT, preferred_element_type=F32)
            for i, value in enumerate((mixed, grad)):
                if prev:
                    value += prev_ref(rest)[i, :, full]
                if last:
                    a, b = value[:half], value[padded : padded + half]
                    outs[0][i, :, cut] = jnp.where(first, a, b)
                    outs[1][i, :, cut] = jnp.where(first, b, a).astype(BF16)
                else:
                    outs[0][i, :, cut] = value

    def prev_ref(rest):
        return rest[0]

    if last:
        shapes = [
            jax.ShapeDtypeStruct((2, half, feats), F32),
            jax.ShapeDtypeStruct((2, half, feats), BF16),
        ]
    else:
        shapes = [jax.ShapeDtypeStruct((2, 2 * padded, feats), F32)]
    return call(
        kernel,
        "down",
        [SMEM] + [VMEM] * (5 + len(prev)),
        shapes,
        [pltpu.VMEM((3, 2 * padded, width), BF16)],
        limit=6,
        estimate=cost(6 * 256 * feats * width, 6 * feats * width),
    )(where, own, other, *[resident(w) for w in weights], *prev)


def fold(keep, got):
    _, n, feats = keep.shape
    half = n // 2

    def kernel(keep, got, stay, send):
        for i in range(2):
            value = keep[i] + got[i].astype(F32)
            stay[i] = value[:half]
            send[i] = value[half:].astype(BF16)

    return call(
        kernel,
        "fold",
        [VMEM] * 2,
        [jax.ShapeDtypeStruct((2, half, feats), F32), jax.ShapeDtypeStruct((2, half, feats), BF16)],
    )(keep, got)


def finish(keeps, gots):
    n = len(keeps)
    _, rows, feats = keeps[0].shape

    def kernel(*refs):
        outs = refs[2 * n :]
        for j in range(n):
            for i in range(2):
                value = refs[j][i] + refs[n + j][i].astype(F32)
                outs[i][:, j * feats : (j + 1) * feats] = value.astype(BF16)

    return call(
        kernel,
        "finish",
        [VMEM] * (2 * n),
        [jax.ShapeDtypeStruct((rows, n * feats), BF16)] * 2,
    )(*keeps, *gots)


def per_device(sizes, tokens, cotangent, gate_weight, up_weight, down_weight):
    grp, blk, bulk = sizes["grp"], sizes["blk"], sizes["bulk"]
    units, feats = gate_weight.shape[1], gate_weight.shape[0]
    split = units % (grp * 128) == 0
    whole = units // grp if split else units
    block = 256 if whole % 256 == 0 else 128
    blocks = whole // block
    cuts = [0, blocks - blocks // 2, blocks] if blocks > 1 else [0, blocks]
    chunks = [(a * block, (b - a) * block) for a, b in zip(cuts, cuts[1:])]
    down_block = 256 if feats % 256 == 0 else 128

    core = lax.axis_index("bulk") % 2
    group = lax.axis_index("grp") if split else jnp.int32(0)
    where = jnp.stack([group, core]).astype(jnp.int32)

    hops = [("blk", blk, b) for b in reversed(bits(blk))]
    if split:
        hops += [("grp", grp, b) for b in bits(grp)]

    gates, ups, downs = (
        [(w, (dim, whole, start, size)) for start, size in chunks]
        for w, dim in ((gate_weight, 1), (up_weight, 1), (down_weight, 0))
    )
    (gate0,) = fetch(where, [gates[0]])
    near = (tokens, cotangent)
    far = tuple(swap(v, *hops[0]) for v in near)
    near = pack(near, far, (gate0,))
    (up0,) = fetch(where, [ups[0]], (near,))
    for hop in hops[1:-1]:
        near = pack((near,), (swap(near, *hop),), (up0,))
    far = swap(near, *hops[-1])
    down0, *more = fetch(where, [downs[0]] + gates[1:], (near,))
    half = near.shape[1]
    padded = -(-half // 16) * 16

    weights = [[gate0, up0, down0]] + [[g, None, None] for g in more]
    summed = []
    after = ()
    for c, w in enumerate(weights):
        later = ups[1:] if c == 0 else downs[c : c + 1]
        keep, send, got = up(where, near, far, 0, w[:2], False, block, later, after)
        if c == 0:
            for v, value in zip(weights[1:], got):
                v[1] = value
        else:
            w[2] = got[0]
        keep_b, send_b, _ = up(where, near, far, 1, w[2:], True, block, (), after)
        keep, send = [*keep, *keep_b], [*send, *send_b]
        sums, rounded = gather(keep, [swap(v, "bulk", bulk, 1) for v in send])
        after = (rounded,)
        summed.append((sums, rounded))

    prev = ()
    for c, (w, (sums, rounded)) in enumerate(zip(weights, summed)):
        for b in bits(bulk, 2)[:-1]:
            sums, rounded = add(sums, swap(rounded, "bulk", bulk, b))
        got = swap(rounded, "bulk", bulk, bits(bulk, 2)[-1])
        own = activate(sums, got, padded, (*prev, *[r for _, r in summed[c + 1 :]]))
        other = swap(own, "bulk", bulk, 1)
        if c < len(chunks) - 1:
            prev = down(where, own, other, w, prev, half, (0, feats), False, down_block)
    pieces = 2 if feats % (2 * down_block) == 0 else 1
    stays, gots = [], []
    for p in range(pieces):
        part = (p * feats // pieces, feats // pieces)
        stay, send = down(where, own, other, w, prev, half, part, True, down_block)
        for hop in reversed(hops[1:]):
            stay, send = fold(stay, swap(send, *hop))
        stays.append(stay)
        gots.append(swap(send, *hops[0]))
    return tuple(finish(stays, gots))


def solution(mesh):
    return jax.shard_map(
        functools.partial(per_device, dict(mesh.shape)),
        mesh=mesh,
        in_specs=(
            P(("grp", "blk"), "bulk"),
            P(("grp", "blk"), "bulk"),
            P("bulk", "blk"),
            P("bulk", "blk"),
            P("blk", "bulk"),
        ),
        out_specs=(P(("grp", "blk"), "bulk"), P(("grp", "blk"), "bulk")),
        check_vma=False,
    )
```

```python
import functools

import jax
import jax.numpy as jnp
from jax import lax
from jax.experimental import pallas as pl
from jax.experimental.pallas import tpu as pltpu
from jax.sharding import PartitionSpec as P

F32 = jnp.float32
BF16 = jnp.bfloat16
NT = (((1,), (1,)), ((), ()))
MIB = 2**20
WINDOWS = [["g0"], ["u0", "g1"], ["d0"]]
BESIDE = {"b0": ["u1"], "gu0": [], "gu1": ["d1"], "b1": []}
FIRST = 0.5
PIECE = 0.5
VMEM = pl.BlockSpec(memory_space=pltpu.VMEM)
SMEM = pl.BlockSpec(memory_space=pltpu.SMEM)
HBM = pl.BlockSpec(memory_space=pltpu.HBM)
ANY = pl.BlockSpec(memory_space=pl.ANY)


def swap(value, axis, size, bit):
    return lax.ppermute(value, axis, [(i, i ^ bit) for i in range(size)])


def bits(size, first=1):
    out = []
    while first < size:
        out.append(first)
        first *= 2
    return out


def resident(x):
    return pltpu.with_memory_space_constraint(x, pltpu.VMEM)


def in_hbm(x):
    return pltpu.with_memory_space_constraint(x, pltpu.HBM)


def cost(flops, nbytes):
    return pl.CostEstimate(flops=flops, bytes_accessed=nbytes, transcendentals=0)


def call(kernel, name, in_specs, out_shape, scratch=(), limit=2, estimate=None):
    many = isinstance(out_shape, (list, tuple))
    return pl.pallas_call(
        kernel,
        in_specs=in_specs,
        out_specs=[VMEM] * len(out_shape) if many else VMEM,
        out_shape=out_shape,
        scratch_shapes=list(scratch),
        compiler_params=pltpu.CompilerParams(vmem_limit_bytes=limit * MIB),
        cost_estimate=estimate,
        name=name,
    )


def copies(where, specs, srcs, outs, sems):
    made = []
    for i, ((dim, whole, start, size), src, out) in enumerate(zip(specs, srcs, outs)):
        first = pl.multiple_of(where[0] * whole + start, 128)
        part = src.at[pl.ds(first, size), :] if dim == 0 else src.at[:, pl.ds(first, size)]
        made.append(pltpu.make_async_copy(part, out, sems.at[i]))
    return made


def fetched(weight, spec):
    shape = list(weight.shape)
    shape[spec[0]] = spec[3]
    return pltpu.VMEM(tuple(shape), BF16)


def fetch(where, wanted, after=()):
    weights, specs = zip(*wanted)
    n = len(wanted)

    def kernel(where, *refs):
        made = copies(where, specs, refs[:n], refs[n + len(after) : -1], refs[-1])
        for copy in made:
            copy.start()
        for copy in made:
            copy.wait()

    outs = [fetched(w, s) for w, s in wanted]
    return call(
        kernel,
        "fetch",
        [SMEM] + [HBM] * n + [ANY] * len(after),
        outs,
        [pltpu.SemaphoreType.DMA((n,))],
        estimate=cost(0, sum(2 * o.shape[0] * o.shape[1] for o in outs)),
    )(where, *[in_hbm(w) for w in weights], *after)


def pack(near, far, after):
    n, feats = near[0].shape
    m = len(near)

    def kernel(*refs):
        outs, wide = refs[-m - 1 : -1], refs[-1]
        for i in range(m):
            wide[i, :n, :] = refs[i][...].astype(F32)
            wide[i, n : 2 * n, :] = refs[m + i][...].astype(F32)
            outs[i][...] = wide[i].astype(BF16)

    return call(
        kernel,
        "pack",
        [VMEM] * (2 * m) + [ANY] * len(after),
        [jax.ShapeDtypeStruct((2 * n, feats), BF16)] * m,
        [pltpu.VMEM((m, 2 * n, feats), F32)],
        limit=2,
    )(*near, *far, *after)


def locate(block, order, count):
    place = 0
    for bit, hop in enumerate(order):
        place += ((block >> hop) & 1) << bit
    return place // (count // 2), place % (count // 2)


def up(where, near, far, order, weights, transposed, block, wanted=(), after=()):
    half, feats = near.shape
    count = 2 ** len(order)
    rows = 2 * half // count
    width = weights[0].shape[0 if transposed else 1]
    n, m = len(weights), len(wanted)
    specs = [s for _, s in wanted]

    def kernel(where, near, far, *refs):
        refs = list(refs)
        ws = [refs.pop(0) for _ in range(n)]
        srcs = [refs.pop(0) for _ in range(m)]
        del refs[: len(after)]
        outs = [refs.pop(0) for _ in range(2 * n)]
        dsts = [refs.pop(0) for _ in range(m)]
        wide, lhs = refs[:2]
        made = copies(where, specs, srcs, dsts, refs[2]) if m else []
        for copy in made:
            copy.start()
        first = where[1] == 0
        both = (near[...].astype(F32), far[...].astype(F32))
        run = half if order == sorted(order) else rows
        for at in range(0, 2 * half, run):
            picks = []
            for start in (at, (at + half) % (2 * half)):
                side, place = locate(start // rows, order, count)
                picks.append(both[side][place * rows : place * rows + run])
            wide[at : at + run, :] = jnp.where(first, *picks)
        lhs[...] = wide[...].astype(BF16)

        def tile(cut):
            for i, w in enumerate(ws):
                if transposed:
                    value = lax.dot_general(lhs[...], w[cut, :], NT, preferred_element_type=F32)
                else:
                    value = jnp.dot(lhs[...], w[:, cut], preferred_element_type=F32)
                outs[2 * i][:, cut] = value[:half]
                outs[2 * i + 1][:, cut] = value[half:]

        if made:
            block2 = width // 2 if width % 256 == 0 else width

            @pl.loop(0, width // block2)
            def _(step):
                tile(pl.ds(pl.multiple_of(step * block2, 128), block2))

        else:
            for step in range(width // block):
                tile(slice(step * block, (step + 1) * block))
        for copy in made:
            copy.wait()

    out = jax.ShapeDtypeStruct((half, width), F32)
    got = call(
        kernel,
        "up",
        [SMEM] + [VMEM] * (2 + n) + [HBM] * m + [ANY] * len(after),
        [out] * (2 * n) + [fetched(w, s) for w, s in wanted],
        [pltpu.VMEM((2 * half, feats), F32), pltpu.VMEM((2 * half, feats), BF16)]
        + ([pltpu.SemaphoreType.DMA((m,))] if m else []),
        limit=2,
        estimate=cost(2 * n * 256 * feats * width, 2 * n * feats * width),
    )(where, near, far, *[resident(w) for w in weights], *[in_hbm(w) for w, _ in wanted], *after)
    return got[: 2 * n : 2], got[1 : 2 * n : 2], got[2 * n :]


def gather(keeps, gots):
    n = len(keeps)
    shape = (n,) + keeps[0].shape

    def kernel(*refs):
        total, rounded = refs[-2:]
        for i in range(n):
            value = refs[i][...] + refs[n + i][...]
            total[i] = value
            rounded[i] = value.astype(BF16)

    return call(
        kernel,
        "gather",
        [VMEM] * (2 * n),
        [jax.ShapeDtypeStruct(shape, F32), jax.ShapeDtypeStruct(shape, BF16)],
    )(*keeps, *gots)


def add(a, b):
    def kernel(a, b, total, rounded):
        value = a[...] + b[...].astype(F32)
        total[...] = value
        rounded[...] = value.astype(BF16)

    return call(
        kernel,
        "add",
        [VMEM] * 2,
        [jax.ShapeDtypeStruct(a.shape, F32), jax.ShapeDtypeStruct(a.shape, BF16)],
    )(a, b)


def activate(sums, got, padded, after):
    _, half, width = sums.shape

    def kernel(sums, got, *rest):
        out = rest[-1]
        gate = sums[0] + got[0].astype(F32)
        upward = sums[1] + got[1].astype(F32)
        back = sums[2] + got[2].astype(F32)
        sigma = jax.nn.sigmoid(gate)
        hidden = gate * sigma * upward
        d_up = back * gate * sigma
        d_gate = back * upward * sigma * (1.0 + gate * (1.0 - sigma))
        for i, value in enumerate((hidden, d_gate, d_up)):
            if padded > half:
                empty = jnp.zeros((padded - half, width), F32)
                value = jnp.concatenate([value, empty], axis=0)
            out[i] = value.astype(BF16)

    return call(
        kernel,
        "activate",
        [VMEM] * 2 + [ANY] * len(after),
        jax.ShapeDtypeStruct((3, padded, width), BF16),
        limit=2,
    )(sums, got, *after)


def down(where, own, other, weights, prev, half, part, last):
    _, padded, width = own.shape
    start, feats = part
    block = 256 if feats % 256 == 0 else 128

    def kernel(where, own, other, gate_w, up_w, down_w, *rest):
        lhs = rest[-1]
        outs = rest[len(prev) : -1]
        first = where[1] == 0
        lhs[:, :padded, :] = own[...]
        lhs[:, padded:, :] = other[...]

        for step in range(feats // block):
            cut = slice(step * block, (step + 1) * block)
            full = slice(start + step * block, start + (step + 1) * block)
            mixed = jnp.dot(lhs[0], down_w[:, full], preferred_element_type=F32)
            grad = lax.dot_general(lhs[1], gate_w[full, :], NT, preferred_element_type=F32)
            grad += lax.dot_general(lhs[2], up_w[full, :], NT, preferred_element_type=F32)
            for i, value in enumerate((mixed, grad)):
                if prev:
                    value += prev_ref(rest)[i, :, full]
                if last:
                    a, b = value[:half], value[padded : padded + half]
                    outs[0][i, :, cut] = jnp.where(first, a, b)
                    outs[1][i, :, cut] = jnp.where(first, b, a).astype(BF16)
                else:
                    outs[0][i, :, cut] = value

    def prev_ref(rest):
        return rest[0]

    if last:
        shapes = [
            jax.ShapeDtypeStruct((2, half, feats), F32),
            jax.ShapeDtypeStruct((2, half, feats), BF16),
        ]
    else:
        shapes = [jax.ShapeDtypeStruct((2, 2 * padded, feats), F32)]
    return call(
        kernel,
        "down",
        [SMEM] + [VMEM] * (5 + len(prev)),
        shapes,
        [pltpu.VMEM((3, 2 * padded, width), BF16)],
        limit=2,
        estimate=cost(6 * 256 * feats * width, 6 * feats * width),
    )(where, own, other, *[resident(w) for w in weights], *prev)


def fold(keep, got):
    _, n, feats = keep.shape
    half = n // 2

    def kernel(keep, got, stay, send):
        for i in range(2):
            value = keep[i] + got[i].astype(F32)
            stay[i] = value[:half]
            send[i] = value[half:].astype(BF16)

    return call(
        kernel,
        "fold",
        [VMEM] * 2,
        [jax.ShapeDtypeStruct((2, half, feats), F32), jax.ShapeDtypeStruct((2, half, feats), BF16)],
    )(keep, got)


def finish(keeps, gots):
    n = len(keeps)
    rows = keeps[0].shape[1]
    sizes = [k.shape[2] for k in keeps]

    def kernel(*refs):
        outs = refs[2 * n :]
        for j, size in enumerate(sizes):
            at = sum(sizes[:j])
            for i in range(2):
                value = refs[j][i] + refs[n + j][i].astype(F32)
                outs[i][:, at : at + size] = value.astype(BF16)

    return call(
        kernel,
        "finish",
        [VMEM] * (2 * n),
        [jax.ShapeDtypeStruct((rows, sum(sizes)), BF16)] * 2,
    )(*keeps, *gots)


def per_device(sizes, tokens, cotangent, gate_weight, up_weight, down_weight):
    grp, blk, bulk = sizes["grp"], sizes["blk"], sizes["bulk"]
    units, feats = gate_weight.shape[1], gate_weight.shape[0]
    split = units % (grp * 128) == 0
    whole = units // grp if split else units
    block = 256 if whole % 256 == 0 else 128
    blocks = whole // block
    cuts = [0, int(blocks * FIRST), blocks] if blocks > 1 else [0, blocks]
    chunks = [(a * block, (b - a) * block) for a, b in zip(cuts, cuts[1:])]
    lead = int(feats * PIECE) // 256 * 256
    pieces = [(0, lead), (lead, feats - lead)] if lead else [(0, feats)]

    core = lax.axis_index("bulk") % 2
    group = lax.axis_index("grp") if split else jnp.int32(0)
    where = jnp.stack([group, core]).astype(jnp.int32)

    hops = [("blk", blk, b) for b in reversed(bits(blk))]
    if split:
        hops += [("grp", grp, b) for b in bits(grp)]

    sources = {"g": (gate_weight, 1), "u": (up_weight, 1), "d": (down_weight, 0)}
    here = {}

    def wanted(names):
        found = []
        for name in names:
            if int(name[1]) < len(chunks):
                weight, dim = sources[name[0]]
                found.append((name, (weight, (dim, whole, *chunks[int(name[1])]))))
        return [n for n, _ in found], [w for _, w in found]

    n = len(hops)
    orders = (list(range(n)), [n - 1, *range(n - 1)])
    near, far = [tokens, cotangent], [None, None]
    after = []
    for step in range(n):
        far = [swap(v, *hops[o[step]]) for v, o in zip(near, orders)]
        names, parts = wanted(WINDOWS[2 if step == n - 1 else step] if step < 2 or step == n - 1 else [])
        got = fetch(where, parts, after) if parts else []
        here.update(zip(names, got))
        if step < n - 1:
            near = pack(near, far, got)
            after = near
    half = near[0].shape[0]
    padded = -(-half // 16) * 16

    summed = []
    after = ()
    for c in range(len(chunks)):
        out = {}
        for kind, i in (("gu", 0), ("b", 1)) if c else (("b", 1), ("gu", 0)):
            ws = [here[f"{w}{c}"] for w in ("d" if kind == "b" else "gu")]
            names, parts = wanted(BESIDE[f"{kind}{c}"])
            *out[kind], got = up(
                where, near[i], far[i], orders[i], ws, kind == "b", block, parts, after
            )
            here.update(zip(names, got))
        keep, send = ([*out["gu"][i], *out["b"][i]] for i in range(2))
        sums, rounded = gather(keep, [swap(v, "bulk", bulk, 1) for v in send])
        after = (rounded,)
        summed.append((sums, rounded))

    prev = ()
    for c, (sums, rounded) in enumerate(summed):
        for b in bits(bulk, 2)[:-1]:
            sums, rounded = add(sums, swap(rounded, "bulk", bulk, b))
        got = swap(rounded, "bulk", bulk, bits(bulk, 2)[-1])
        w = [here[f"{name}{c}"] for name in "gud"]
        own = activate(sums, got, padded, (*prev, *[r for _, r in summed[c + 1 :]]))
        other = swap(own, "bulk", bulk, 1)
        if c < len(chunks) - 1:
            prev = down(where, own, other, w, prev, half, (0, feats), False)
    stays, gots = [], []
    for part in pieces:
        stay, send = down(where, own, other, w, prev, half, part, True)
        for hop in reversed(hops[1:]):
            stay, send = fold(stay, swap(send, *hop))
        stays.append(stay)
        gots.append(swap(send, *hops[0]))
    return tuple(finish(stays, gots))


def solution(mesh):
    return jax.shard_map(
        functools.partial(per_device, dict(mesh.shape)),
        mesh=mesh,
        in_specs=(
            P(("grp", "blk"), "bulk"),
            P(("grp", "blk"), "bulk"),
            P("bulk", "blk"),
            P("bulk", "blk"),
            P("blk", "bulk"),
        ),
        out_specs=(P(("grp", "blk"), "bulk"), P(("grp", "blk"), "bulk")),
        check_vma=False,
    )
```

```python
import functools

import jax
import jax.numpy as jnp
from jax import lax
from jax.experimental import pallas as pl
from jax.experimental.pallas import tpu as pltpu
from jax.sharding import PartitionSpec as P

F32 = jnp.float32
BF16 = jnp.bfloat16
NT = (((1,), (1,)), ((), ()))
MIB = 2**20
WINDOWS = [["g0"], ["u0", "g1"], ["d0"]]
BESIDE = {"b0": ["u1"], "gu0": [], "gu1": ["d1"], "b1": []}
FIRST = 0.62
EST = 1
PARTS = [1, 1]
ORDER = 0
SPLITS = [0.5]
SENDS = [1, 2]
VMEM = pl.BlockSpec(memory_space=pltpu.VMEM)
SMEM = pl.BlockSpec(memory_space=pltpu.SMEM)
HBM = pl.BlockSpec(memory_space=pltpu.HBM)
ANY = pl.BlockSpec(memory_space=pl.ANY)


def swap(value, axis, size, bit):
    return lax.ppermute(value, axis, [(i, i ^ bit) for i in range(size)])


def bits(size, first=1):
    out = []
    while first < size:
        out.append(first)
        first *= 2
    return out


def resident(x):
    return pltpu.with_memory_space_constraint(x, pltpu.VMEM)


def in_hbm(x):
    return pltpu.with_memory_space_constraint(x, pltpu.HBM)


def cost(flops, nbytes):
    return pl.CostEstimate(flops=flops, bytes_accessed=nbytes, transcendentals=0)


def call(kernel, name, in_specs, out_shape, scratch=(), limit=2, estimate=None):
    many = isinstance(out_shape, (list, tuple))
    return pl.pallas_call(
        kernel,
        in_specs=in_specs,
        out_specs=[VMEM] * len(out_shape) if many else VMEM,
        out_shape=out_shape,
        scratch_shapes=list(scratch),
        compiler_params=pltpu.CompilerParams(vmem_limit_bytes=limit * MIB),
        cost_estimate=estimate,
        name=name,
    )


def copies(where, specs, srcs, outs, sems):
    made = []
    for i, ((dim, whole, start, size), src, out) in enumerate(zip(specs, srcs, outs)):
        first = pl.multiple_of(where[0] * whole + start, 128)
        part = src.at[pl.ds(first, size), :] if dim == 0 else src.at[:, pl.ds(first, size)]
        made.append(pltpu.make_async_copy(part, out, sems.at[i]))
    return made


def fetched(weight, spec):
    shape = list(weight.shape)
    shape[spec[0]] = spec[3]
    return pltpu.VMEM(tuple(shape), BF16)


def fetch(where, wanted, after=()):
    weights, specs = zip(*wanted)
    n = len(wanted)

    def kernel(where, *refs):
        made = copies(where, specs, refs[:n], refs[n + len(after) : -1], refs[-1])
        for copy in made:
            copy.start()
        for copy in made:
            copy.wait()

    outs = [fetched(w, s) for w, s in wanted]
    return call(
        kernel,
        "fetch",
        [SMEM] + [HBM] * n + [ANY] * len(after),
        outs,
        [pltpu.SemaphoreType.DMA((n,))],
        estimate=cost(0, sum(2 * o.shape[0] * o.shape[1] for o in outs)),
    )(where, *[in_hbm(w) for w in weights], *after)


def pack(near, far, after):
    n, feats = near[0].shape
    m = len(near)

    def kernel(*refs):
        outs, wide = refs[-m - 1 : -1], refs[-1]
        for i in range(m):
            wide[i, :n, :] = refs[i][...].astype(F32)
            wide[i, n : 2 * n, :] = refs[m + i][...].astype(F32)
            outs[i][...] = wide[i].astype(BF16)

    return call(
        kernel,
        "pack",
        [VMEM] * (2 * m) + [ANY] * len(after),
        [jax.ShapeDtypeStruct((2 * n, feats), BF16)] * m,
        [pltpu.VMEM((m, 2 * n, feats), F32)],
        limit=2,
    )(*near, *far, *after)


def locate(block, order, count):
    place = 0
    for bit, hop in enumerate(order):
        place += ((block >> hop) & 1) << bit
    return place // (count // 2), place % (count // 2)


def up(where, near, far, order, weights, transposed, block, cuts, wanted=(), after=()):
    half, feats = near.shape
    count = 2 ** len(order)
    rows = 2 * half // count
    width = weights[0].shape[0 if transposed else 1]
    n, m = len(weights), len(wanted)
    specs = [s for _, s in wanted]

    def kernel(where, near, far, *refs):
        refs = list(refs)
        ws = [refs.pop(0) for _ in range(n)]
        srcs = [refs.pop(0) for _ in range(m)]
        del refs[: len(after)]
        outs = [[refs.pop(0) for _ in range(len(cuts))] for _ in range(n)]
        dsts = [refs.pop(0) for _ in range(m)]
        wide, lhs = refs[:2]
        made = copies(where, specs, srcs, dsts, refs[2]) if m else []
        for copy in made:
            copy.start()
        first = where[1] == 0
        both = (near[...].astype(F32), far[...].astype(F32))
        run = half if order == sorted(order) else rows
        for at in range(0, 2 * half, run):
            picks = []
            for start in (at, (at + half) % (2 * half)):
                side, place = locate(start // rows, order, count)
                picks.append(both[side][place * rows : place * rows + run])
            wide[at : at + run, :] = jnp.where(first, *picks)
        lhs[...] = wide[...].astype(BF16)

        def tile(cut):
            for i, w in enumerate(ws):
                if transposed:
                    value = lax.dot_general(lhs[...], w[cut, :], NT, preferred_element_type=F32)
                else:
                    value = jnp.dot(lhs[...], w[:, cut], preferred_element_type=F32)
                for out, (start, size) in zip(outs[i], cuts):
                    out[:, cut] = value[start : start + size]

        if made:
            block2 = width // 2 if width % 256 == 0 else width

            @pl.loop(0, width // block2)
            def _(step):
                tile(pl.ds(pl.multiple_of(step * block2, 128), block2))

        else:
            for step in range(width // block):
                tile(slice(step * block, (step + 1) * block))
        for copy in made:
            copy.wait()

    shapes = [jax.ShapeDtypeStruct((size, width), F32) for _, size in cuts] * n
    got = call(
        kernel,
        "up",
        [SMEM] + [VMEM] * (2 + n) + [HBM] * m + [ANY] * len(after),
        shapes + [fetched(w, s) for w, s in wanted],
        [pltpu.VMEM((2 * half, feats), F32), pltpu.VMEM((2 * half, feats), BF16)]
        + ([pltpu.SemaphoreType.DMA((m,))] if m else []),
        limit=2,
        estimate=cost(2 * n * 256 * feats * width, 2 * n * feats * width),
    )(where, near, far, *[resident(w) for w in weights], *[in_hbm(w) for w, _ in wanted], *after)
    k = len(cuts)
    return [got[i * k : (i + 1) * k] for i in range(n)], got[n * k :]


def gather(keeps, gots, cuts):
    n, m = len(keeps), len(gots[0])
    rows = keeps[0].shape[0]

    def kernel(*refs):
        outs = refs[n + n * m :]
        for k, (start, width) in enumerate(cuts):
            at = slice(start, start + width)
            for i in range(n):
                top = 0
                for got in refs[n + i * m : n + (i + 1) * m]:
                    run = slice(top, top + got.shape[0])
                    value = refs[i][run, at] + got[:, at]
                    outs[2 * k][i, run] = value
                    outs[2 * k + 1][i, run] = value.astype(BF16)
                    top += got.shape[0]

    outs = call(
        kernel,
        "gather",
        [VMEM] * (n + n * m),
        [jax.ShapeDtypeStruct((n, rows, w), t) for _, w in cuts for t in (F32, BF16)],
    )(*keeps, *[v for got in gots for v in got])
    return list(zip(outs[::2], outs[1::2]))


def add(a, b):
    def kernel(a, b, total, rounded):
        value = a[...] + b[...].astype(F32)
        total[...] = value
        rounded[...] = value.astype(BF16)

    return call(
        kernel,
        "add",
        [VMEM] * 2,
        [jax.ShapeDtypeStruct(a.shape, F32), jax.ShapeDtypeStruct(a.shape, BF16)],
    )(a, b)


def activate(sums, got, padded, after):
    _, half, width = sums.shape

    def kernel(sums, got, *rest):
        outs = rest[-3:]
        gate = sums[0] + got[0].astype(F32)
        upward = sums[1] + got[1].astype(F32)
        back = sums[2] + got[2].astype(F32)
        sigma = jax.nn.sigmoid(gate)
        hidden = gate * sigma * upward
        d_up = back * gate * sigma
        d_gate = back * upward * sigma * (1.0 + gate * (1.0 - sigma))
        for out, value in zip(outs, (hidden, d_gate, d_up)):
            if padded > half:
                empty = jnp.zeros((padded - half, width), F32)
                value = jnp.concatenate([value, empty], axis=0)
            out[...] = value.astype(BF16)

    return call(
        kernel,
        "activate",
        [VMEM] * 2 + [ANY] * len(after),
        [jax.ShapeDtypeStruct((padded, width), BF16)] * 3,
        limit=2,
    )(sums, got, *after)


def down(where, own, other, weights, units, prev, half, part, last):
    padded, width = own[0].shape
    start, feats = part
    units = slice(units[0], units[0] + units[1])
    block = 256 if feats % 256 == 0 else 128

    def kernel(where, *rest):
        own, other, (gate_w, up_w, down_w), rest = rest[:3], rest[3:6], rest[6:9], rest[9:]
        lhs = rest[-1]
        outs = rest[len(prev) : -1]
        first = where[1] == 0
        for i in range(3):
            lhs[i, :padded, :] = own[i][...]
            lhs[i, padded:, :] = other[i][...]

        for step in range(feats // block):
            cut = slice(step * block, (step + 1) * block)
            full = slice(start + step * block, start + (step + 1) * block)
            mixed = jnp.dot(lhs[0], down_w[units, full], preferred_element_type=F32)
            grad = lax.dot_general(lhs[1], gate_w[full, units], NT, preferred_element_type=F32)
            grad += lax.dot_general(lhs[2], up_w[full, units], NT, preferred_element_type=F32)
            for i, value in enumerate((mixed, grad)):
                if prev:
                    value += prev_ref(rest)[i, :, full]
                if last:
                    a, b = value[:half], value[padded : padded + half]
                    outs[0][i, :, cut] = jnp.where(first, a, b)
                    outs[1][i, :, cut] = jnp.where(first, b, a).astype(BF16)
                else:
                    outs[0][i, :, cut] = value

    def prev_ref(rest):
        return rest[0]

    if last:
        shapes = [
            jax.ShapeDtypeStruct((2, half, feats), F32),
            jax.ShapeDtypeStruct((2, half, feats), BF16),
        ]
    else:
        shapes = [jax.ShapeDtypeStruct((2, 2 * padded, feats), F32)]
    return call(
        kernel,
        "down",
        [SMEM] + [VMEM] * (9 + len(prev)),
        shapes,
        [pltpu.VMEM((3, 2 * padded, width), BF16)],
        limit=2,
        estimate=cost(6 * 256 * feats * width, 6 * feats * width) if last else cost(EST, EST),
    )(where, *own, *other, *[resident(w) for w in weights], *prev)


def fold(keep, got, after):
    _, n, feats = keep.shape
    half = n // 2

    def kernel(keep, got, *rest):
        stay, send = rest[-2:]
        for i in range(2):
            value = keep[i] + got[i].astype(F32)
            stay[i] = value[:half]
            send[i] = value[half:].astype(BF16)

    return call(
        kernel,
        "fold",
        [VMEM] * 2 + [ANY] * len(after),
        [jax.ShapeDtypeStruct((2, half, feats), F32), jax.ShapeDtypeStruct((2, half, feats), BF16)],
    )(keep, got, *after)


def finish(keeps, gots):
    n = len(keeps)
    rows = keeps[0].shape[1]
    sizes = [k.shape[2] for k in keeps]

    def kernel(*refs):
        outs = refs[2 * n :]
        for j, size in enumerate(sizes):
            at = sum(sizes[:j])
            for i in range(2):
                value = refs[j][i] + refs[n + j][i].astype(F32)
                outs[i][:, at : at + size] = value.astype(BF16)

    return call(
        kernel,
        "finish",
        [VMEM] * (2 * n),
        [jax.ShapeDtypeStruct((rows, sum(sizes)), BF16)] * 2,
    )(*keeps, *gots)


def per_device(sizes, tokens, cotangent, gate_weight, up_weight, down_weight):
    grp, blk, bulk = sizes["grp"], sizes["blk"], sizes["bulk"]
    units, feats = gate_weight.shape[1], gate_weight.shape[0]
    split = units % (grp * 128) == 0
    whole = units // grp if split else units
    block = 256 if whole % 256 == 0 else 128
    blocks = whole // block
    cuts = [0, int(blocks * FIRST), blocks] if blocks > 1 else [0, blocks]
    chunks = [(a * block, (b - a) * block) for a, b in zip(cuts, cuts[1:])]
    ends = [0, *[int(feats * v) // 256 * 256 for v in SPLITS], feats]
    pieces = [(a, b - a) for a, b in zip(ends, ends[1:]) if b > a]

    core = lax.axis_index("bulk") % 2
    group = lax.axis_index("grp") if split else jnp.int32(0)
    where = jnp.stack([group, core]).astype(jnp.int32)

    hops = [("blk", blk, b) for b in reversed(bits(blk))]
    if split:
        hops += [("grp", grp, b) for b in bits(grp)]

    sources = {"g": (gate_weight, 1), "u": (up_weight, 1), "d": (down_weight, 0)}
    here = {}

    def wanted(names):
        found = []
        for name in names:
            if int(name[1]) < len(chunks):
                weight, dim = sources[name[0]]
                found.append((name, (weight, (dim, whole, *chunks[int(name[1])]))))
        return [n for n, _ in found], [w for _, w in found]

    n = len(hops)
    orders = (list(range(n)), [[n - 1, *range(n - 1)], [0, n - 1, *range(1, n - 1)]][ORDER])
    near, far = [tokens, cotangent], [None, None]
    after = []
    for step in range(n):
        far = [swap(v, *hops[o[step]]) for v, o in zip(near, orders)]
        names, parts = wanted(WINDOWS[2 if step == n - 1 else step] if step < 2 or step == n - 1 else [])
        got = fetch(where, parts, after) if parts else []
        here.update(zip(names, got))
        if step < n - 1:
            near = pack(near, far, got)
            after = near
    half = near[0].shape[0]
    padded = -(-half // 16) * 16

    summed = []
    after = ()
    for c in range(len(chunks)):
        out = {}
        top = -(-half // 32) * 16 if SENDS[c] == 2 else half
        runs = [(0, half), (half, top)] + ([(half + top, half - top)] if top < half else [])
        for kind, i in (("gu", 0), ("b", 1)) if c else (("b", 1), ("gu", 0)):
            ws = [here[f"{w}{c}"] for w in ("d" if kind == "b" else "gu")]
            names, parts = wanted(BESIDE[f"{kind}{c}"])
            out[kind], got = up(
                where, near[i], far[i], orders[i], ws, kind == "b", block, runs, parts, after
            )
            here.update(zip(names, got))
        out = out["gu"] + out["b"]
        size = chunks[c][1]
        parts = PARTS[c] if size % (128 * PARTS[c]) == 0 else 1
        cuts = [(i * size // parts, size // parts) for i in range(parts)]
        sums = gather(
            [v[0] for v in out], [[swap(r, "bulk", bulk, 1) for r in v[1:]] for v in out], cuts
        )
        after = tuple(rounded for _, rounded in sums)
        summed += [(c, cut, *pair) for cut, pair in zip(cuts, sums)]

    prev = ()
    for step, (c, cut, sums, rounded) in enumerate(summed):
        for b in bits(bulk, 2)[:-1]:
            sums, rounded = add(sums, swap(rounded, "bulk", bulk, b))
        got = swap(rounded, "bulk", bulk, bits(bulk, 2)[-1])
        w = [here[f"{name}{c}"] for name in "gud"]
        own = activate(sums, got, padded, (*prev, *[v[-1] for v in summed[step + 1 :]]))
        other = [swap(v, "bulk", bulk, 1) for v in own]
        if step < len(summed) - 1:
            prev = down(where, own, other, w, cut, prev, half, (0, feats), False)
    made = [down(where, own, other, w, cut, prev, half, part, True) for part in pieces]
    stays, gots = [], []
    for p, (stay, send) in enumerate(made):
        late = made[p + 1][1:] if p + 1 < len(made) else ()
        for hop in reversed(hops[1:]):
            stay, send = fold(stay, swap(send, *hop), late)
            late = ()
        stays.append(stay)
        gots.append(swap(send, *hops[0]))
    return tuple(finish(stays, gots))


def solution(mesh):
    return jax.shard_map(
        functools.partial(per_device, dict(mesh.shape)),
        mesh=mesh,
        in_specs=(
            P(("grp", "blk"), "bulk"),
            P(("grp", "blk"), "bulk"),
            P("bulk", "blk"),
            P("bulk", "blk"),
            P("blk", "bulk"),
        ),
        out_specs=(P(("grp", "blk"), "bulk"), P(("grp", "blk"), "bulk")),
        check_vma=False,
    )
```

```python
import functools

import jax
import jax.numpy as jnp
from jax import lax
from jax.experimental import pallas as pl
from jax.experimental.pallas import tpu as pltpu
from jax.sharding import PartitionSpec as P

F32 = jnp.float32
BF16 = jnp.bfloat16
NT = (((1,), (1,)), ((), ()))
MIB = 2**20
WINDOWS = [["g0"], ["u0", "g1"], ["d0"]]
BESIDE = [[["d", ["u1"]], ["gu", ["d1"]]], [["gud", []]]]
UPLIM = 3
INNER = True
FIRST = 0.54
EST = 1
PARTS = [1, 2]
ORDER = 0
SPLITS = [0.38]
SENDS = [1, 2]
VMEM = pl.BlockSpec(memory_space=pltpu.VMEM)
SMEM = pl.BlockSpec(memory_space=pltpu.SMEM)
HBM = pl.BlockSpec(memory_space=pltpu.HBM)
ANY = pl.BlockSpec(memory_space=pl.ANY)


def swap(value, axis, size, bit):
    return lax.ppermute(value, axis, [(i, i ^ bit) for i in range(size)])


def bits(size, first=1):
    out = []
    while first < size:
        out.append(first)
        first *= 2
    return out


def resident(x):
    return pltpu.with_memory_space_constraint(x, pltpu.VMEM)


def in_hbm(x):
    return pltpu.with_memory_space_constraint(x, pltpu.HBM)


def cost(flops, nbytes):
    return pl.CostEstimate(flops=flops, bytes_accessed=nbytes, transcendentals=0)


def call(kernel, name, in_specs, out_shape, scratch=(), limit=2, estimate=None):
    many = isinstance(out_shape, (list, tuple))
    return pl.pallas_call(
        kernel,
        in_specs=in_specs,
        out_specs=[VMEM] * len(out_shape) if many else VMEM,
        out_shape=out_shape,
        scratch_shapes=list(scratch),
        compiler_params=pltpu.CompilerParams(vmem_limit_bytes=limit * MIB),
        cost_estimate=estimate,
        name=name,
    )


def copies(where, specs, srcs, outs, sems):
    made = []
    for i, ((dim, whole, start, size), src, out) in enumerate(zip(specs, srcs, outs)):
        first = pl.multiple_of(where[0] * whole + start, 128)
        part = src.at[pl.ds(first, size), :] if dim == 0 else src.at[:, pl.ds(first, size)]
        made.append(pltpu.make_async_copy(part, out, sems.at[i]))
    return made


def fetched(weight, spec):
    shape = list(weight.shape)
    shape[spec[0]] = spec[3]
    return pltpu.VMEM(tuple(shape), BF16)


def fetch(where, wanted, after=()):
    weights, specs = zip(*wanted)
    n = len(wanted)

    def kernel(where, *refs):
        made = copies(where, specs, refs[:n], refs[n + len(after) : -1], refs[-1])
        for copy in made:
            copy.start()
        for copy in made:
            copy.wait()

    outs = [fetched(w, s) for w, s in wanted]
    return call(
        kernel,
        "fetch",
        [SMEM] + [HBM] * n + [ANY] * len(after),
        outs,
        [pltpu.SemaphoreType.DMA((n,))],
        estimate=cost(0, sum(2 * o.shape[0] * o.shape[1] for o in outs)),
    )(where, *[in_hbm(w) for w in weights], *after)


def pack(near, far, after):
    n, feats = near[0].shape
    m = len(near)

    def kernel(*refs):
        outs, wide = refs[-m - 1 : -1], refs[-1]
        for i in range(m):
            wide[i, :n, :] = refs[i][...].astype(F32)
            wide[i, n : 2 * n, :] = refs[m + i][...].astype(F32)
            outs[i][...] = wide[i].astype(BF16)

    return call(
        kernel,
        "pack",
        [VMEM] * (2 * m) + [ANY] * len(after),
        [jax.ShapeDtypeStruct((2 * n, feats), BF16)] * m,
        [pltpu.VMEM((m, 2 * n, feats), F32)],
        limit=2,
    )(*near, *far, *after)


def locate(block, order, count):
    place = 0
    for bit, hop in enumerate(order):
        place += ((block >> hop) & 1) << bit
    return place // (count // 2), place % (count // 2)


def up(where, kinds, nears, fars, orders, weights, block, cuts, wanted=(), after=()):
    sides = sorted({int(kind == "d") for kind in kinds})
    nears, fars, orders = ([v[i] for i in sides] for v in (nears, fars, orders))
    n, k = len(sides), len(kinds)
    half, feats = nears[0].shape
    count = 2 ** len(orders[0])
    rows = 2 * half // count
    width = weights[0].shape[0 if kinds[0] == "d" else 1]
    m = len(wanted)
    specs = [s for _, s in wanted]

    def kernel(where, *refs):
        refs = list(refs)
        near, far = ([refs.pop(0) for _ in sides] for _ in range(2))
        ws = [refs.pop(0) for _ in kinds]
        srcs = [refs.pop(0) for _ in range(m)]
        del refs[: len(after)]
        outs = [[refs.pop(0) for _ in cuts] for _ in kinds]
        dsts = [refs.pop(0) for _ in range(m)]
        wide, lhs = refs[:2]
        made = copies(where, specs, srcs, dsts, refs[2]) if m else []
        for copy in made:
            copy.start()
        first = where[1] == 0
        for i, order in enumerate(orders):
            both = (near[i][...].astype(F32), far[i][...].astype(F32))
            run = half if order == sorted(order) else rows
            for at in range(0, 2 * half, run):
                picks = []
                for start in (at, (at + half) % (2 * half)):
                    side, place = locate(start // rows, order, count)
                    picks.append(both[side][place * rows : place * rows + run])
                wide[at : at + run, :] = jnp.where(first, *picks)
            lhs[i] = wide[...].astype(BF16)

        def tile(cut):
            for kind, w, out in zip(kinds, ws, outs):
                if kind == "d":
                    value = lax.dot_general(
                        lhs[n - 1], w[cut, :], NT, preferred_element_type=F32
                    )
                else:
                    value = jnp.dot(lhs[0], w[:, cut], preferred_element_type=F32)
                for ref, (start, size) in zip(out, cuts):
                    ref[:, cut] = value[start : start + size]

        if made:
            large = width // 2 if width % 256 == 0 else width

            @pl.loop(0, width // large)
            def _(step):
                tile(pl.ds(pl.multiple_of(step * large, 128), large))

        else:
            for step in range(width // block):
                tile(slice(step * block, (step + 1) * block))
        for copy in made:
            copy.wait()

    shapes = [jax.ShapeDtypeStruct((size, width), F32) for _, size in cuts] * k
    got = call(
        kernel,
        "up",
        [SMEM] + [VMEM] * (2 * n + k) + [HBM] * m + [ANY] * len(after),
        shapes + [fetched(w, s) for w, s in wanted],
        [pltpu.VMEM((2 * half, feats), F32), pltpu.VMEM((n, 2 * half, feats), BF16)]
        + ([pltpu.SemaphoreType.DMA((m,))] if m else []),
        limit=UPLIM,
        estimate=cost(2 * k * 256 * feats * width, 2 * k * feats * width),
    )(
        where,
        *nears,
        *fars,
        *[resident(w) for w in weights],
        *[in_hbm(w) for w, _ in wanted],
        *after,
    )
    r = len(cuts)
    return [got[i * r : (i + 1) * r] for i in range(k)], got[k * r :]


def gather(keeps, gots, cuts):
    n, m = len(keeps), len(gots[0])
    rows = keeps[0].shape[0]

    def kernel(*refs):
        outs = refs[n + n * m :]
        for k, (start, width) in enumerate(cuts):
            at = slice(start, start + width)
            for i in range(n):
                top = 0
                for got in refs[n + i * m : n + (i + 1) * m]:
                    run = slice(top, top + got.shape[0])
                    value = refs[i][run, at] + got[:, at]
                    outs[2 * k][i, run] = value
                    outs[2 * k + 1][i, run] = value.astype(BF16)
                    top += got.shape[0]

    outs = call(
        kernel,
        "gather",
        [VMEM] * (n + n * m),
        [jax.ShapeDtypeStruct((n, rows, w), t) for _, w in cuts for t in (F32, BF16)],
    )(*keeps, *[v for got in gots for v in got])
    return list(zip(outs[::2], outs[1::2]))


def add(a, b):
    def kernel(a, b, total, rounded):
        value = a[...] + b[...].astype(F32)
        total[...] = value
        rounded[...] = value.astype(BF16)

    return call(
        kernel,
        "add",
        [VMEM] * 2,
        [jax.ShapeDtypeStruct(a.shape, F32), jax.ShapeDtypeStruct(a.shape, BF16)],
    )(a, b)


def activate(sums, gots, padded, after):
    n, half = len(sums), sums[0].shape[1]
    widths = [v.shape[2] for v in sums]

    def kernel(*refs):
        outs = refs[-3:]
        for p, width in enumerate(widths):
            gate, upward, back = (refs[p][i] + refs[n + p][i].astype(F32) for i in range(3))
            sigma = jax.nn.sigmoid(gate)
            hidden = gate * sigma * upward
            d_up = back * gate * sigma
            d_gate = back * upward * sigma * (1.0 + gate * (1.0 - sigma))
            at = sum(widths[:p])
            for out, value in zip(outs, (hidden, d_gate, d_up)):
                if padded > half:
                    empty = jnp.zeros((padded - half, width), F32)
                    value = jnp.concatenate([value, empty], axis=0)
                out[:, at : at + width] = value.astype(BF16)

    return call(
        kernel,
        "activate",
        [VMEM] * (2 * n) + [ANY] * len(after),
        [jax.ShapeDtypeStruct((padded, sum(widths)), BF16)] * 3,
        limit=3,
    )(*sums, *gots, *after)


def down(where, own, other, weights, prev, half, part, last, inner=False):
    padded, width = own[0].shape
    start, feats = part
    block = 256 if feats % 256 == 0 else 128

    def kernel(where, *rest):
        own, other, (gate_w, up_w, down_w), rest = rest[:3], rest[3:6], rest[6:9], rest[9:]
        lhs, swapped = rest[-2:]
        outs = rest[len(prev) : -2]
        first = where[1] == 0
        for i in range(3):
            lhs[i, :padded, :] = own[i][...]
            lhs[i, padded:, :] = other[i][...]

        for step in range(feats // block):
            cut = slice(step * block, (step + 1) * block)
            full = slice(start + step * block, start + (step + 1) * block)
            mixed = jnp.dot(lhs[0], down_w[:, full], preferred_element_type=F32)
            grad = lax.dot_general(lhs[1], gate_w[full, :], NT, preferred_element_type=F32)
            grad += lax.dot_general(lhs[2], up_w[full, :], NT, preferred_element_type=F32)
            for i, value in enumerate((mixed, grad)):
                if prev:
                    value += prev_ref(rest)[i, :, full]
                if last:
                    a, b = value[:half], value[padded : padded + half]
                    a, b = jnp.where(first, a, b), jnp.where(first, b, a)
                    if inner:
                        q = half // 2
                        for at, rows in ((0, a), (q, b)):
                            outs[0][i, at : at + q, cut] = rows[:q]
                            swapped[i, at : at + q, :] = rows[q:]
                        outs[1][i, :, cut] = swapped[i].astype(BF16)
                    else:
                        outs[0][i, :, cut] = a
                        outs[1][i, :, cut] = b.astype(BF16)
                else:
                    outs[0][i, :, cut] = value

    def prev_ref(rest):
        return rest[0]

    if last:
        shapes = [
            jax.ShapeDtypeStruct((2, half, feats), F32),
            jax.ShapeDtypeStruct((2, half, feats), BF16),
        ]
    else:
        shapes = [jax.ShapeDtypeStruct((2, 2 * padded, feats), F32)]
    return call(
        kernel,
        "down",
        [SMEM] + [VMEM] * (9 + len(prev)),
        shapes,
        [pltpu.VMEM((3, 2 * padded, width), BF16), pltpu.VMEM((2, half, block), F32)],
        limit=2,
        estimate=cost(6 * 256 * feats * width, 6 * feats * width) if last else cost(EST, EST),
    )(where, *own, *other, *[resident(w) for w in weights], *prev)


def fold(keep, got, after):
    _, n, feats = keep.shape
    half = n // 2

    def kernel(keep, got, *rest):
        stay, send = rest[-2:]
        for i in range(2):
            value = keep[i] + got[i].astype(F32)
            stay[i] = value[:half]
            send[i] = value[half:].astype(BF16)

    return call(
        kernel,
        "fold",
        [VMEM] * 2 + [ANY] * len(after),
        [jax.ShapeDtypeStruct((2, half, feats), F32), jax.ShapeDtypeStruct((2, half, feats), BF16)],
    )(keep, got, *after)


def finish(keeps, gots):
    n = len(keeps)
    rows = keeps[0].shape[1]
    sizes = [k.shape[2] for k in keeps]

    def kernel(*refs):
        outs = refs[2 * n :]
        for j, size in enumerate(sizes):
            at = sum(sizes[:j])
            for i in range(2):
                value = refs[j][i] + refs[n + j][i].astype(F32)
                outs[i][:, at : at + size] = value.astype(BF16)

    return call(
        kernel,
        "finish",
        [VMEM] * (2 * n),
        [jax.ShapeDtypeStruct((rows, sum(sizes)), BF16)] * 2,
    )(*keeps, *gots)


def per_device(sizes, tokens, cotangent, gate_weight, up_weight, down_weight):
    grp, blk, bulk = sizes["grp"], sizes["blk"], sizes["bulk"]
    units, feats = gate_weight.shape[1], gate_weight.shape[0]
    split = units % (grp * 128) == 0
    whole = units // grp if split else units
    block = 256 if whole % 256 == 0 else 128
    blocks = whole // block
    cuts = [0, int(blocks * FIRST), blocks] if blocks > 1 else [0, blocks]
    chunks = [(a * block, (b - a) * block) for a, b in zip(cuts, cuts[1:])]
    ends = [0, *[int(feats * v) // 256 * 256 for v in SPLITS], feats]
    pieces = [(a, b - a) for a, b in zip(ends, ends[1:]) if b > a]

    core = lax.axis_index("bulk") % 2
    group = lax.axis_index("grp") if split else jnp.int32(0)
    where = jnp.stack([group, core]).astype(jnp.int32)

    hops = [("blk", blk, b) for b in reversed(bits(blk))]
    if split:
        hops += [("grp", grp, b) for b in bits(grp)]

    sources = {"g": (gate_weight, 1), "u": (up_weight, 1), "d": (down_weight, 0)}
    here = {}

    def wanted(names):
        found = []
        for name in names:
            if int(name[1]) < len(chunks):
                weight, dim = sources[name[0]]
                found.append((name, (weight, (dim, whole, *chunks[int(name[1])]))))
        return [n for n, _ in found], [w for _, w in found]

    n = len(hops)
    orders = (list(range(n)), [[n - 1, *range(n - 1)], [0, n - 1, *range(1, n - 1)]][ORDER])
    near, far = [tokens, cotangent], [None, None]
    after = []
    for step in range(n):
        far = [swap(v, *hops[o[step]]) for v, o in zip(near, orders)]
        names, parts = wanted(WINDOWS[2 if step == n - 1 else step] if step < 2 or step == n - 1 else [])
        got = fetch(where, parts, after) if parts else []
        here.update(zip(names, got))
        if step < n - 1:
            near = pack(near, far, got)
            after = near
    half = near[0].shape[0]
    padded = -(-half // 16) * 16

    summed = []
    after = ()
    for c in range(len(chunks)):
        step = -(-half // (8 * SENDS[c])) * 8
        runs = [(0, half)] + [(half + t, min(step, half - t)) for t in range(0, half, step)]
        out = {}
        for kinds, beside in BESIDE[c]:
            ws = [here[f"{w}{c}"] for w in kinds]
            names, parts = wanted(beside)
            made, got = up(where, kinds, near, far, orders, ws, block, runs, parts, after)
            here.update(zip(names, got))
            out.update(zip(kinds, made))
        out = [out[kind] for kind in "gud"]
        size = chunks[c][1]
        parts = PARTS[c] if size % (128 * PARTS[c]) == 0 else 1
        cuts = [(i * size // parts, size // parts) for i in range(parts)]
        sums = gather(
            [v[0] for v in out], [[swap(r, "bulk", bulk, 1) for r in v[1:]] for v in out], cuts
        )
        after = tuple(rounded for _, rounded in sums)
        summed.append(sums)

    prev = ()
    for c, pairs in enumerate(summed):
        sums, gots = [], []
        for total, rounded in pairs:
            for b in bits(bulk, 2)[:-1]:
                total, rounded = add(total, swap(rounded, "bulk", bulk, b))
            sums.append(total)
            gots.append(swap(rounded, "bulk", bulk, bits(bulk, 2)[-1]))
        w = [here[f"{name}{c}"] for name in "gud"]
        late = [r for later in summed[c + 1 :] for _, r in later]
        own = activate(sums, gots, padded, (*prev, *late))
        other = [swap(v, "bulk", bulk, 1) for v in own]
        if c < len(chunks) - 1:
            prev = down(where, own, other, w, prev, half, (0, feats), False)
    made = [
        down(where, own, other, w, prev, half, part, True, INNER and p == 1)
        for p, part in enumerate(pieces)
    ]
    stays, gots = [], []
    for p, (stay, send) in enumerate(made):
        late = made[p + 1][1:] if p + 1 < len(made) else ()
        path = hops[::-1]
        if INNER and p == 1:
            path = [path[1], path[0], *path[2:]]
        for hop in path[:-1]:
            stay, send = fold(stay, swap(send, *hop), late)
            late = ()
        stays.append(stay)
        gots.append(swap(send, *path[-1]))
    return tuple(finish(stays, gots))


def solution(mesh):
    return jax.shard_map(
        functools.partial(per_device, dict(mesh.shape)),
        mesh=mesh,
        in_specs=(
            P(("grp", "blk"), "bulk"),
            P(("grp", "blk"), "bulk"),
            P("bulk", "blk"),
            P("bulk", "blk"),
            P("blk", "bulk"),
        ),
        out_specs=(P(("grp", "blk"), "bulk"), P(("grp", "blk"), "bulk")),
        check_vma=False,
    )
```

```python
import functools

import jax
import jax.numpy as jnp
from jax import lax
from jax.experimental import pallas as pl
from jax.experimental.pallas import tpu as pltpu
from jax.sharding import PartitionSpec as P

F32 = jnp.float32
BF16 = jnp.bfloat16
NT = (((1,), (1,)), ((), ()))
MIB = 2**20
WINDOWS = [["g0"], ["u0", "g1"], ["d0"]]
BESIDE = [[["d", ["u1"]], ["gu", ["d1"]]], [["gud", []]]]
UPLIM = 3
INNER = True
FIRST = 0.54
EST = 1
PARTS = [1, 2]
SPLITS = [0.38]
SENDS = [1, 2]
VMEM = pl.BlockSpec(memory_space=pltpu.VMEM)
SMEM = pl.BlockSpec(memory_space=pltpu.SMEM)
HBM = pl.BlockSpec(memory_space=pltpu.HBM)
ANY = pl.BlockSpec(memory_space=pl.ANY)


def swap(value, axis, size, bit):
    return lax.ppermute(value, axis, [(i, i ^ bit) for i in range(size)])


def bits(size, first=1):
    out = []
    while first < size:
        out.append(first)
        first *= 2
    return out


def resident(x):
    return pltpu.with_memory_space_constraint(x, pltpu.VMEM)


def in_hbm(x):
    return pltpu.with_memory_space_constraint(x, pltpu.HBM)


def cost(flops, nbytes):
    return pl.CostEstimate(flops=flops, bytes_accessed=nbytes, transcendentals=0)


def call(kernel, name, in_specs, out_shape, scratch=(), limit=2, estimate=None):
    many = isinstance(out_shape, (list, tuple))
    return pl.pallas_call(
        kernel,
        in_specs=in_specs,
        out_specs=[VMEM] * len(out_shape) if many else VMEM,
        out_shape=out_shape,
        scratch_shapes=list(scratch),
        compiler_params=pltpu.CompilerParams(vmem_limit_bytes=limit * MIB),
        cost_estimate=estimate,
        name=name,
    )


def copies(where, specs, srcs, outs, sems):
    made = []
    for i, ((dim, whole, start, size), src, out) in enumerate(zip(specs, srcs, outs)):
        first = pl.multiple_of(where[0] * whole + start, 128)
        part = src.at[pl.ds(first, size), :] if dim == 0 else src.at[:, pl.ds(first, size)]
        made.append(pltpu.make_async_copy(part, out, sems.at[i]))
    return made


def fetched(weight, spec):
    shape = list(weight.shape)
    shape[spec[0]] = spec[3]
    return pltpu.VMEM(tuple(shape), BF16)


def fetch(where, wanted, after=()):
    weights, specs = zip(*wanted)
    n = len(wanted)

    def kernel(where, *refs):
        made = copies(where, specs, refs[:n], refs[n + len(after) : -1], refs[-1])
        for copy in made:
            copy.start()
        for copy in made:
            copy.wait()

    outs = [fetched(w, s) for w, s in wanted]
    return call(
        kernel,
        "fetch",
        [SMEM] + [HBM] * n + [ANY] * len(after),
        outs,
        [pltpu.SemaphoreType.DMA((n,))],
        estimate=cost(0, sum(2 * o.shape[0] * o.shape[1] for o in outs)),
    )(where, *[in_hbm(w) for w in weights], *after)


def pack(near, far, after):
    n, feats = near[0].shape
    m = len(near)

    def kernel(*refs):
        outs, wide = refs[-m - 1 : -1], refs[-1]
        for i in range(m):
            wide[i, :n, :] = refs[i][...].astype(F32)
            wide[i, n : 2 * n, :] = refs[m + i][...].astype(F32)
            outs[i][...] = wide[i].astype(BF16)

    return call(
        kernel,
        "pack",
        [VMEM] * (2 * m) + [ANY] * len(after),
        [jax.ShapeDtypeStruct((2 * n, feats), BF16)] * m,
        [pltpu.VMEM((m, 2 * n, feats), F32)],
        limit=2,
    )(*near, *far, *after)


def locate(block, order, count):
    place = 0
    for bit, hop in enumerate(order):
        place += ((block >> hop) & 1) << bit
    return place // (count // 2), place % (count // 2)


def up(where, kinds, nears, fars, orders, weights, block, cuts, wanted=(), after=()):
    sides = sorted({int(kind == "d") for kind in kinds})
    nears, fars, orders = ([v[i] for i in sides] for v in (nears, fars, orders))
    n, k = len(sides), len(kinds)
    half, feats = nears[0].shape
    count = 2 ** len(orders[0])
    rows = 2 * half // count
    width = weights[0].shape[0 if kinds[0] == "d" else 1]
    m = len(wanted)
    specs = [s for _, s in wanted]

    def kernel(where, *refs):
        refs = list(refs)
        near, far = ([refs.pop(0) for _ in sides] for _ in range(2))
        ws = [refs.pop(0) for _ in kinds]
        srcs = [refs.pop(0) for _ in range(m)]
        del refs[: len(after)]
        outs = [[refs.pop(0) for _ in cuts] for _ in kinds]
        dsts = [refs.pop(0) for _ in range(m)]
        wide, lhs = refs[:2]
        made = copies(where, specs, srcs, dsts, refs[2]) if m else []
        for copy in made:
            copy.start()
        first = where[1] == 0
        for i, order in enumerate(orders):
            both = (near[i][...].astype(F32), far[i][...].astype(F32))
            run = half if order == sorted(order) else rows
            for at in range(0, 2 * half, run):
                picks = []
                for start in (at, (at + half) % (2 * half)):
                    side, place = locate(start // rows, order, count)
                    picks.append(both[side][place * rows : place * rows + run])
                wide[at : at + run, :] = jnp.where(first, *picks)
            lhs[i] = wide[...].astype(BF16)

        def tile(cut):
            for kind, w, out in zip(kinds, ws, outs):
                if kind == "d":
                    value = lax.dot_general(
                        lhs[n - 1], w[cut, :], NT, preferred_element_type=F32
                    )
                else:
                    value = jnp.dot(lhs[0], w[:, cut], preferred_element_type=F32)
                for ref, (start, size) in zip(out, cuts):
                    ref[:, cut] = value[start : start + size]

        if made:
            large = width // 2 if width % 256 == 0 else width

            @pl.loop(0, width // large)
            def _(step):
                tile(pl.ds(pl.multiple_of(step * large, 128), large))

        else:
            for step in range(width // block):
                tile(slice(step * block, (step + 1) * block))
        for copy in made:
            copy.wait()

    shapes = [jax.ShapeDtypeStruct((size, width), F32) for _, size in cuts] * k
    got = call(
        kernel,
        "up",
        [SMEM] + [VMEM] * (2 * n + k) + [HBM] * m + [ANY] * len(after),
        shapes + [fetched(w, s) for w, s in wanted],
        [pltpu.VMEM((2 * half, feats), F32), pltpu.VMEM((n, 2 * half, feats), BF16)]
        + ([pltpu.SemaphoreType.DMA((m,))] if m else []),
        limit=UPLIM,
        estimate=cost(2 * k * 256 * feats * width, 2 * k * feats * width),
    )(
        where,
        *nears,
        *fars,
        *[resident(w) for w in weights],
        *[in_hbm(w) for w, _ in wanted],
        *after,
    )
    r = len(cuts)
    return [got[i * r : (i + 1) * r] for i in range(k)], got[k * r :]


def gather(keeps, gots, cuts):
    n, m = len(keeps), len(gots[0])
    rows = keeps[0].shape[0]

    def kernel(*refs):
        outs = refs[n + n * m :]
        for k, (start, width) in enumerate(cuts):
            at = slice(start, start + width)
            for i in range(n):
                top = 0
                for got in refs[n + i * m : n + (i + 1) * m]:
                    run = slice(top, top + got.shape[0])
                    outs[2 * k][i, run] = refs[i][run, at] + got[:, at]
                    top += got.shape[0]
                outs[2 * k + 1][i] = outs[2 * k][i].astype(BF16)

    outs = call(
        kernel,
        "gather",
        [VMEM] * (n + n * m),
        [jax.ShapeDtypeStruct((n, rows, w), t) for _, w in cuts for t in (F32, BF16)],
    )(*keeps, *[v for got in gots for v in got])
    return list(zip(outs[::2], outs[1::2]))


def add(a, b):
    def kernel(a, b, total, rounded):
        value = a[...] + b[...].astype(F32)
        total[...] = value
        rounded[...] = value.astype(BF16)

    return call(
        kernel,
        "add",
        [VMEM] * 2,
        [jax.ShapeDtypeStruct(a.shape, F32), jax.ShapeDtypeStruct(a.shape, BF16)],
    )(a, b)


def activate(sums, gots, padded, after):
    n, half = len(sums), sums[0].shape[1]
    widths = [v.shape[2] for v in sums]

    def kernel(*refs):
        outs = refs[-3:]
        for p, width in enumerate(widths):
            gate, upward, back = (refs[p][i] + refs[n + p][i].astype(F32) for i in range(3))
            sigma = jax.nn.sigmoid(gate)
            hidden = gate * sigma * upward
            d_up = back * gate * sigma
            d_gate = back * upward * sigma * (1.0 + gate * (1.0 - sigma))
            at = sum(widths[:p])
            for out, value in zip(outs, (hidden, d_gate, d_up)):
                if padded > half:
                    empty = jnp.zeros((padded - half, width), F32)
                    value = jnp.concatenate([value, empty], axis=0)
                out[:, at : at + width] = value.astype(BF16)

    return call(
        kernel,
        "activate",
        [VMEM] * (2 * n) + [ANY] * len(after),
        [jax.ShapeDtypeStruct((padded, sum(widths)), BF16)] * 3,
        limit=3,
    )(*sums, *gots, *after)


def down(where, own, other, weights, prev, half, part, last, inner=False):
    padded, width = own[0].shape
    start, feats = part
    block = 256 if feats % 256 == 0 else 128

    def kernel(where, *rest):
        own, other, (gate_w, up_w, down_w), rest = rest[:3], rest[3:6], rest[6:9], rest[9:]
        lhs, swapped = rest[-2:]
        outs = rest[len(prev) : -2]
        first = where[1] == 0
        for i in range(3):
            lhs[i, :padded, :] = own[i][...]
            lhs[i, padded:, :] = other[i][...]

        for step in range(feats // block):
            cut = slice(step * block, (step + 1) * block)
            full = slice(start + step * block, start + (step + 1) * block)
            mixed = jnp.dot(lhs[0], down_w[:, full], preferred_element_type=F32)
            grad = lax.dot_general(lhs[1], gate_w[full, :], NT, preferred_element_type=F32)
            grad += lax.dot_general(lhs[2], up_w[full, :], NT, preferred_element_type=F32)
            for i, value in enumerate((mixed, grad)):
                if prev:
                    value += prev_ref(rest)[i, :, full]
                if last:
                    a, b = value[:half], value[padded : padded + half]
                    a, b = jnp.where(first, a, b), jnp.where(first, b, a)
                    if inner:
                        q = half // 2
                        for at, rows in ((0, a), (q, b)):
                            outs[0][i, at : at + q, cut] = rows[:q]
                            swapped[i, at : at + q, :] = rows[q:]
                        outs[1][i, :, cut] = swapped[i].astype(BF16)
                    else:
                        outs[0][i, :, cut] = a
                        outs[1][i, :, cut] = b.astype(BF16)
                else:
                    outs[0][i, :, cut] = value

    def prev_ref(rest):
        return rest[0]

    if last:
        shapes = [
            jax.ShapeDtypeStruct((2, half, feats), F32),
            jax.ShapeDtypeStruct((2, half, feats), BF16),
        ]
    else:
        shapes = [jax.ShapeDtypeStruct((2, 2 * padded, feats), F32)]
    return call(
        kernel,
        "down",
        [SMEM] + [VMEM] * (9 + len(prev)),
        shapes,
        [pltpu.VMEM((3, 2 * padded, width), BF16), pltpu.VMEM((2, half, block), F32)],
        limit=2,
        estimate=cost(6 * 256 * feats * width, 6 * feats * width) if last else cost(EST, EST),
    )(where, *own, *other, *[resident(w) for w in weights], *prev)


def fold(keep, got, after):
    _, n, feats = keep.shape
    half = n // 2

    def kernel(keep, got, *rest):
        stay, send = rest[-2:]
        for i in range(2):
            value = keep[i] + got[i].astype(F32)
            stay[i] = value[:half]
            send[i] = value[half:].astype(BF16)

    return call(
        kernel,
        "fold",
        [VMEM] * 2 + [ANY] * len(after),
        [jax.ShapeDtypeStruct((2, half, feats), F32), jax.ShapeDtypeStruct((2, half, feats), BF16)],
    )(keep, got, *after)


def finish(keeps, gots):
    n = len(keeps)
    rows = keeps[0].shape[1]
    sizes = [k.shape[2] for k in keeps]

    def kernel(*refs):
        outs = refs[2 * n :]
        for j, size in enumerate(sizes):
            at = sum(sizes[:j])
            for i in range(2):
                value = refs[j][i] + refs[n + j][i].astype(F32)
                outs[i][:, at : at + size] = value.astype(BF16)

    return call(
        kernel,
        "finish",
        [VMEM] * (2 * n),
        [jax.ShapeDtypeStruct((rows, sum(sizes)), BF16)] * 2,
    )(*keeps, *gots)


def per_device(sizes, tokens, cotangent, gate_weight, up_weight, down_weight):
    grp, blk, bulk = sizes["grp"], sizes["blk"], sizes["bulk"]
    units, feats = gate_weight.shape[1], gate_weight.shape[0]
    split = units % (grp * 128) == 0
    whole = units // grp if split else units
    block = 256 if whole % 256 == 0 else 128
    blocks = whole // block
    cuts = [0, int(blocks * FIRST), blocks] if blocks > 1 else [0, blocks]
    chunks = [(a * block, (b - a) * block) for a, b in zip(cuts, cuts[1:])]
    ends = [0, *[int(feats * v) // 256 * 256 for v in SPLITS], feats]
    pieces = [(a, b - a) for a, b in zip(ends, ends[1:]) if b > a]

    core = lax.axis_index("bulk") % 2
    group = lax.axis_index("grp") if split else jnp.int32(0)
    where = jnp.stack([group, core]).astype(jnp.int32)

    hops = [("blk", blk, b) for b in reversed(bits(blk))]
    if split:
        hops += [("grp", grp, b) for b in bits(grp)]

    sources = {"g": (gate_weight, 1), "u": (up_weight, 1), "d": (down_weight, 0)}
    here = {}

    def wanted(names):
        found = []
        for name in names:
            if int(name[1]) < len(chunks):
                weight, dim = sources[name[0]]
                found.append((name, (weight, (dim, whole, *chunks[int(name[1])]))))
        return [n for n, _ in found], [w for _, w in found]

    n = len(hops)
    orders = (list(range(n)), [n - 1, *range(n - 1)])
    near, far = [tokens, cotangent], [None, None]
    after = []
    for step in range(n):
        far = [swap(v, *hops[o[step]]) for v, o in zip(near, orders)]
        names, parts = wanted(WINDOWS[2 if step == n - 1 else step] if step < 2 or step == n - 1 else [])
        got = fetch(where, parts, after) if parts else []
        here.update(zip(names, got))
        if step < n - 1:
            near = pack(near, far, got)
            after = near
    half = near[0].shape[0]
    padded = -(-half // 16) * 16

    summed = []
    after = ()
    for c in range(len(chunks)):
        step = -(-half // (8 * SENDS[c])) * 8
        runs = [(0, half)] + [(half + t, min(step, half - t)) for t in range(0, half, step)]
        out = {}
        for kinds, beside in BESIDE[c]:
            ws = [here[f"{w}{c}"] for w in kinds]
            names, parts = wanted(beside)
            made, got = up(where, kinds, near, far, orders, ws, block, runs, parts, after)
            here.update(zip(names, got))
            out.update(zip(kinds, made))
        out = [out[kind] for kind in "gud"]
        size = chunks[c][1]
        parts = PARTS[c] if size % (128 * PARTS[c]) == 0 else 1
        cuts = [(i * size // parts, size // parts) for i in range(parts)]
        sums = gather(
            [v[0] for v in out], [[swap(r, "bulk", bulk, 1) for r in v[1:]] for v in out], cuts
        )
        after = tuple(rounded for _, rounded in sums)
        summed.append(sums)

    prev = ()
    for c, pairs in enumerate(summed):
        sums, gots = [], []
        for total, rounded in pairs:
            for b in bits(bulk, 2)[:-1]:
                total, rounded = add(total, swap(rounded, "bulk", bulk, b))
            sums.append(total)
            gots.append(swap(rounded, "bulk", bulk, bits(bulk, 2)[-1]))
        w = [here[f"{name}{c}"] for name in "gud"]
        late = [r for later in summed[c + 1 :] for _, r in later]
        own = activate(sums, gots, padded, (*prev, *late))
        other = [swap(v, "bulk", bulk, 1) for v in own]
        if c < len(chunks) - 1:
            prev = down(where, own, other, w, prev, half, (0, feats), False)
    made = [
        down(where, own, other, w, prev, half, part, True, INNER and p == 1)
        for p, part in enumerate(pieces)
    ]
    stays, gots = [], []
    for p, (stay, send) in enumerate(made):
        late = made[p + 1][1:] if p + 1 < len(made) else ()
        path = hops[::-1]
        if INNER and p == 1:
            path = [path[1], path[0], *path[2:]]
        for hop in path[:-1]:
            stay, send = fold(stay, swap(send, *hop), late)
            late = ()
        stays.append(stay)
        gots.append(swap(send, *path[-1]))
    return tuple(finish(stays, gots))


def solution(mesh):
    return jax.shard_map(
        functools.partial(per_device, dict(mesh.shape)),
        mesh=mesh,
        in_specs=(
            P(("grp", "blk"), "bulk"),
            P(("grp", "blk"), "bulk"),
            P("bulk", "blk"),
            P("bulk", "blk"),
            P("blk", "bulk"),
        ),
        out_specs=(P(("grp", "blk"), "bulk"), P(("grp", "blk"), "bulk")),
        check_vma=False,
    )
```

```python
import functools

import jax
import jax.numpy as jnp
from jax import lax
from jax.experimental import pallas as pl
from jax.experimental.pallas import tpu as pltpu
from jax.sharding import PartitionSpec as P

F32 = jnp.float32
BF16 = jnp.bfloat16
NT = (((1,), (1,)), ((), ()))
MIB = 2**20
WINDOWS = [["g1"], ["u0", "g0"], ["d0"]]
BESIDE = [[["d", ["u1"]], ["gu", ["d1"]]], [["gud", []]]]
UPLIM = 3
INNER = True
FIRST = 0.54
EST = 1
PARTS = [1, 2]
SPLITS = [0.38]
SENDS = [1, 2]
VMEM = pl.BlockSpec(memory_space=pltpu.VMEM)
SMEM = pl.BlockSpec(memory_space=pltpu.SMEM)
HBM = pl.BlockSpec(memory_space=pltpu.HBM)
ANY = pl.BlockSpec(memory_space=pl.ANY)


def swap(value, axis, size, bit):
    return lax.ppermute(value, axis, [(i, i ^ bit) for i in range(size)])


def bits(size, first=1):
    out = []
    while first < size:
        out.append(first)
        first *= 2
    return out


def resident(x):
    return pltpu.with_memory_space_constraint(x, pltpu.VMEM)


def in_hbm(x):
    return pltpu.with_memory_space_constraint(x, pltpu.HBM)


def cost(flops, nbytes):
    return pl.CostEstimate(flops=flops, bytes_accessed=nbytes, transcendentals=0)


def call(kernel, name, in_specs, out_shape, scratch=(), limit=2, estimate=None):
    many = isinstance(out_shape, (list, tuple))
    return pl.pallas_call(
        kernel,
        in_specs=in_specs,
        out_specs=[VMEM] * len(out_shape) if many else VMEM,
        out_shape=out_shape,
        scratch_shapes=list(scratch),
        compiler_params=pltpu.CompilerParams(vmem_limit_bytes=limit * MIB),
        cost_estimate=estimate,
        name=name,
    )


def copies(where, specs, srcs, outs, sems):
    made = []
    for i, ((dim, whole, start, size), src, out) in enumerate(zip(specs, srcs, outs)):
        first = pl.multiple_of(where[0] * whole + start, 128)
        part = src.at[pl.ds(first, size), :] if dim == 0 else src.at[:, pl.ds(first, size)]
        made.append(pltpu.make_async_copy(part, out, sems.at[i]))
    return made


def fetched(weight, spec):
    shape = list(weight.shape)
    shape[spec[0]] = spec[3]
    return pltpu.VMEM(tuple(shape), BF16)


def fetch(where, wanted, after=()):
    weights, specs = zip(*wanted)
    n = len(wanted)

    def kernel(where, *refs):
        made = copies(where, specs, refs[:n], refs[n + len(after) : -1], refs[-1])
        for copy in made:
            copy.start()
        for copy in made:
            copy.wait()

    outs = [fetched(w, s) for w, s in wanted]
    return call(
        kernel,
        "fetch",
        [SMEM] + [HBM] * n + [ANY] * len(after),
        outs,
        [pltpu.SemaphoreType.DMA((n,))],
        estimate=cost(0, sum(2 * o.shape[0] * o.shape[1] for o in outs)),
    )(where, *[in_hbm(w) for w in weights], *after)


def pack(near, far, after):
    n, feats = near[0].shape
    m = len(near)

    def kernel(*refs):
        outs, wide = refs[-m - 1 : -1], refs[-1]
        for i in range(m):
            wide[i, :n, :] = refs[i][...].astype(F32)
            wide[i, n : 2 * n, :] = refs[m + i][...].astype(F32)
            outs[i][...] = wide[i].astype(BF16)

    return call(
        kernel,
        "pack",
        [VMEM] * (2 * m) + [ANY] * len(after),
        [jax.ShapeDtypeStruct((2 * n, feats), BF16)] * m,
        [pltpu.VMEM((m, 2 * n, feats), F32)],
        limit=2,
    )(*near, *far, *after)


def locate(block, order, count):
    place = 0
    for bit, hop in enumerate(order):
        place += ((block >> hop) & 1) << bit
    return place // (count // 2), place % (count // 2)


def up(where, kinds, nears, fars, orders, weights, block, cuts, wanted=(), after=()):
    sides = sorted({int(kind == "d") for kind in kinds})
    nears, fars, orders = ([v[i] for i in sides] for v in (nears, fars, orders))
    n, k = len(sides), len(kinds)
    half, feats = nears[0].shape
    count = 2 ** len(orders[0])
    rows = 2 * half // count
    width = weights[0].shape[0 if kinds[0] == "d" else 1]
    m = len(wanted)
    specs = [s for _, s in wanted]

    def kernel(where, *refs):
        refs = list(refs)
        near, far = ([refs.pop(0) for _ in sides] for _ in range(2))
        ws = [refs.pop(0) for _ in kinds]
        srcs = [refs.pop(0) for _ in range(m)]
        del refs[: len(after)]
        outs = [[refs.pop(0) for _ in cuts] for _ in kinds]
        dsts = [refs.pop(0) for _ in range(m)]
        wide, lhs = refs[:2]
        made = copies(where, specs, srcs, dsts, refs[2]) if m else []
        for copy in made:
            copy.start()
        first = where[1] == 0
        for i, order in enumerate(orders):
            both = (near[i][...].astype(F32), far[i][...].astype(F32))
            run = half if order == sorted(order) else rows
            for at in range(0, 2 * half, run):
                picks = []
                for start in (at, (at + half) % (2 * half)):
                    side, place = locate(start // rows, order, count)
                    picks.append(both[side][place * rows : place * rows + run])
                wide[at : at + run, :] = jnp.where(first, *picks)
            lhs[i] = wide[...].astype(BF16)

        def tile(cut):
            for kind, w, out in zip(kinds, ws, outs):
                if kind == "d":
                    value = lax.dot_general(
                        lhs[n - 1], w[cut, :], NT, preferred_element_type=F32
                    )
                else:
                    value = jnp.dot(lhs[0], w[:, cut], preferred_element_type=F32)
                for ref, (start, size) in zip(out, cuts):
                    ref[:, cut] = value[start : start + size]

        if made:
            large = width // 2 if width % 256 == 0 else width

            @pl.loop(0, width // large)
            def _(step):
                tile(pl.ds(pl.multiple_of(step * large, 128), large))

        else:
            for step in range(width // block):
                tile(slice(step * block, (step + 1) * block))
        for copy in made:
            copy.wait()

    shapes = [jax.ShapeDtypeStruct((size, width), F32) for _, size in cuts] * k
    got = call(
        kernel,
        "up",
        [SMEM] + [VMEM] * (2 * n + k) + [HBM] * m + [ANY] * len(after),
        shapes + [fetched(w, s) for w, s in wanted],
        [pltpu.VMEM((2 * half, feats), F32), pltpu.VMEM((n, 2 * half, feats), BF16)]
        + ([pltpu.SemaphoreType.DMA((m,))] if m else []),
        limit=UPLIM,
        estimate=cost(2 * k * 256 * feats * width, 2 * k * feats * width),
    )(
        where,
        *nears,
        *fars,
        *[resident(w) for w in weights],
        *[in_hbm(w) for w, _ in wanted],
        *after,
    )
    r = len(cuts)
    return [got[i * r : (i + 1) * r] for i in range(k)], got[k * r :]


def gather(keeps, gots, cuts):
    n, m = len(keeps), len(gots[0])
    rows = keeps[0].shape[0]

    def kernel(*refs):
        outs = refs[n + n * m :]
        for k, (start, width) in enumerate(cuts):
            at = slice(start, start + width)
            for i in range(n):
                top = 0
                for got in refs[n + i * m : n + (i + 1) * m]:
                    run = slice(top, top + got.shape[0])
                    outs[2 * k][i, run] = refs[i][run, at] + got[:, at]
                    top += got.shape[0]
                outs[2 * k + 1][i] = outs[2 * k][i].astype(BF16)

    outs = call(
        kernel,
        "gather",
        [VMEM] * (n + n * m),
        [jax.ShapeDtypeStruct((n, rows, w), t) for _, w in cuts for t in (F32, BF16)],
    )(*keeps, *[v for got in gots for v in got])
    return list(zip(outs[::2], outs[1::2]))


def add(a, b):
    def kernel(a, b, total, rounded):
        value = a[...] + b[...].astype(F32)
        total[...] = value
        rounded[...] = value.astype(BF16)

    return call(
        kernel,
        "add",
        [VMEM] * 2,
        [jax.ShapeDtypeStruct(a.shape, F32), jax.ShapeDtypeStruct(a.shape, BF16)],
    )(a, b)


def activate(sums, gots, padded, after):
    n, half = len(sums), sums[0].shape[1]
    widths = [v.shape[2] for v in sums]

    def kernel(*refs):
        outs = refs[-3:]
        for p, width in enumerate(widths):
            gate, upward, back = (refs[p][i] + refs[n + p][i].astype(F32) for i in range(3))
            sigma = jax.nn.sigmoid(gate)
            hidden = gate * sigma * upward
            d_up = back * gate * sigma
            d_gate = back * upward * sigma * (1.0 + gate * (1.0 - sigma))
            at = sum(widths[:p])
            for out, value in zip(outs, (hidden, d_gate, d_up)):
                if padded > half:
                    empty = jnp.zeros((padded - half, width), F32)
                    value = jnp.concatenate([value, empty], axis=0)
                out[:, at : at + width] = value.astype(BF16)

    return call(
        kernel,
        "activate",
        [VMEM] * (2 * n) + [ANY] * len(after),
        [jax.ShapeDtypeStruct((padded, sum(widths)), BF16)] * 3,
        limit=3,
    )(*sums, *gots, *after)


def down(where, own, other, weights, prev, half, part, last, inner=False):
    padded, width = own[0].shape
    start, feats = part
    block = 256 if feats % 256 == 0 else 128

    def kernel(where, *rest):
        own, other, (gate_w, up_w, down_w), rest = rest[:3], rest[3:6], rest[6:9], rest[9:]
        lhs, swapped = rest[-2:]
        outs = rest[len(prev) : -2]
        first = where[1] == 0
        for i in range(3):
            lhs[i, :padded, :] = own[i][...]
            lhs[i, padded:, :] = other[i][...]

        for step in range(feats // block):
            cut = slice(step * block, (step + 1) * block)
            full = slice(start + step * block, start + (step + 1) * block)
            mixed = jnp.dot(lhs[0], down_w[:, full], preferred_element_type=F32)
            grad = lax.dot_general(lhs[1], gate_w[full, :], NT, preferred_element_type=F32)
            grad += lax.dot_general(lhs[2], up_w[full, :], NT, preferred_element_type=F32)
            for i, value in enumerate((mixed, grad)):
                if prev:
                    value += prev_ref(rest)[i, :, full]
                if last:
                    a, b = value[:half], value[padded : padded + half]
                    a, b = jnp.where(first, a, b), jnp.where(first, b, a)
                    if inner:
                        q = half // 2
                        for at, rows in ((0, a), (q, b)):
                            outs[0][i, at : at + q, cut] = rows[:q]
                            swapped[i, at : at + q, :] = rows[q:]
                        outs[1][i, :, cut] = swapped[i].astype(BF16)
                    else:
                        outs[0][i, :, cut] = a
                        outs[1][i, :, cut] = b.astype(BF16)
                else:
                    outs[0][i, :, cut] = value

    def prev_ref(rest):
        return rest[0]

    if last:
        shapes = [
            jax.ShapeDtypeStruct((2, half, feats), F32),
            jax.ShapeDtypeStruct((2, half, feats), BF16),
        ]
    else:
        shapes = [jax.ShapeDtypeStruct((2, 2 * padded, feats), F32)]
    return call(
        kernel,
        "down",
        [SMEM] + [VMEM] * (9 + len(prev)),
        shapes,
        [pltpu.VMEM((3, 2 * padded, width), BF16), pltpu.VMEM((2, half, block), F32)],
        limit=2,
        estimate=cost(6 * 256 * feats * width, 6 * feats * width) if last else cost(EST, EST),
    )(where, *own, *other, *[resident(w) for w in weights], *prev)


def fold(keep, got, after):
    _, n, feats = keep.shape
    half = n // 2

    def kernel(keep, got, *rest):
        stay, send = rest[-2:]
        for i in range(2):
            value = keep[i] + got[i].astype(F32)
            stay[i] = value[:half]
            send[i] = value[half:].astype(BF16)

    return call(
        kernel,
        "fold",
        [VMEM] * 2 + [ANY] * len(after),
        [jax.ShapeDtypeStruct((2, half, feats), F32), jax.ShapeDtypeStruct((2, half, feats), BF16)],
    )(keep, got, *after)


def finish(keeps, gots):
    n = len(keeps)
    rows = keeps[0].shape[1]
    sizes = [k.shape[2] for k in keeps]

    def kernel(*refs):
        outs = refs[2 * n :]
        for j, size in enumerate(sizes):
            at = sum(sizes[:j])
            for i in range(2):
                value = refs[j][i] + refs[n + j][i].astype(F32)
                outs[i][:, at : at + size] = value.astype(BF16)

    return call(
        kernel,
        "finish",
        [VMEM] * (2 * n),
        [jax.ShapeDtypeStruct((rows, sum(sizes)), BF16)] * 2,
    )(*keeps, *gots)


def per_device(sizes, tokens, cotangent, gate_weight, up_weight, down_weight):
    grp, blk, bulk = sizes["grp"], sizes["blk"], sizes["bulk"]
    units, feats = gate_weight.shape[1], gate_weight.shape[0]
    split = units % (grp * 128) == 0
    whole = units // grp if split else units
    block = 256 if whole % 256 == 0 else 128
    blocks = whole // block
    cuts = [0, int(blocks * FIRST), blocks] if blocks > 1 else [0, blocks]
    chunks = [(a * block, (b - a) * block) for a, b in zip(cuts, cuts[1:])]
    ends = [0, *[int(feats * v) // 256 * 256 for v in SPLITS], feats]
    pieces = [(a, b - a) for a, b in zip(ends, ends[1:]) if b > a]

    core = lax.axis_index("bulk") % 2
    group = lax.axis_index("grp") if split else jnp.int32(0)
    where = jnp.stack([group, core]).astype(jnp.int32)

    hops = [("blk", blk, b) for b in reversed(bits(blk))]
    if split:
        hops += [("grp", grp, b) for b in bits(grp)]

    sources = {"g": (gate_weight, 1), "u": (up_weight, 1), "d": (down_weight, 0)}
    here = {}

    def wanted(names):
        found = []
        for name in names:
            if int(name[1]) < len(chunks):
                weight, dim = sources[name[0]]
                found.append((name, (weight, (dim, whole, *chunks[int(name[1])]))))
        return [n for n, _ in found], [w for _, w in found]

    n = len(hops)
    orders = (list(range(n)), [n - 1, *range(n - 1)])
    near, far = [tokens, cotangent], [None, None]
    after = []
    for step in range(n):
        far = [swap(v, *hops[o[step]]) for v, o in zip(near, orders)]
        names, parts = wanted(WINDOWS[2 if step == n - 1 else step] if step < 2 or step == n - 1 else [])
        got = fetch(where, parts, after) if parts else []
        here.update(zip(names, got))
        if step < n - 1:
            near = pack(near, far, got)
            after = near
    half = near[0].shape[0]
    padded = -(-half // 16) * 16

    summed = []
    after = ()
    for c in range(len(chunks)):
        step = -(-half // (8 * SENDS[c])) * 8
        runs = [(0, half)] + [(half + t, min(step, half - t)) for t in range(0, half, step)]
        out = {}
        for kinds, beside in BESIDE[c]:
            ws = [here[f"{w}{c}"] for w in kinds]
            names, parts = wanted(beside)
            made, got = up(where, kinds, near, far, orders, ws, block, runs, parts, after)
            here.update(zip(names, got))
            out.update(zip(kinds, made))
        out = [out[kind] for kind in "gud"]
        size = chunks[c][1]
        parts = PARTS[c] if size % (128 * PARTS[c]) == 0 else 1
        cuts = [(i * size // parts, size // parts) for i in range(parts)]
        sums = gather(
            [v[0] for v in out], [[swap(r, "bulk", bulk, 1) for r in v[1:]] for v in out], cuts
        )
        after = tuple(rounded for _, rounded in sums)
        summed.append(sums)

    prev = ()
    for c, pairs in enumerate(summed):
        sums, gots = [], []
        for total, rounded in pairs:
            for b in bits(bulk, 2)[:-1]:
                total, rounded = add(total, swap(rounded, "bulk", bulk, b))
            sums.append(total)
            gots.append(swap(rounded, "bulk", bulk, bits(bulk, 2)[-1]))
        w = [here[f"{name}{c}"] for name in "gud"]
        late = [r for later in summed[c + 1 :] for _, r in later]
        own = activate(sums, gots, padded, (*prev, *late))
        other = [swap(v, "bulk", bulk, 1) for v in own]
        if c < len(chunks) - 1:
            prev = down(where, own, other, w, prev, half, (0, feats), False)
    made = [
        down(where, own, other, w, prev, half, part, True, INNER and p == 1)
        for p, part in enumerate(pieces)
    ]
    stays, gots = [], []
    for p, (stay, send) in enumerate(made):
        late = made[p + 1][1:] if p + 1 < len(made) else ()
        path = hops[::-1]
        if INNER and p == 1:
            path = [path[1], path[0], *path[2:]]
        for hop in path[:-1]:
            stay, send = fold(stay, swap(send, *hop), late)
            late = ()
        stays.append(stay)
        gots.append(swap(send, *path[-1]))
    return tuple(finish(stays, gots))


def solution(mesh):
    return jax.shard_map(
        functools.partial(per_device, dict(mesh.shape)),
        mesh=mesh,
        in_specs=(
            P(("grp", "blk"), "bulk"),
            P(("grp", "blk"), "bulk"),
            P("bulk", "blk"),
            P("bulk", "blk"),
            P("blk", "bulk"),
        ),
        out_specs=(P(("grp", "blk"), "bulk"), P(("grp", "blk"), "bulk")),
        check_vma=False,
    )
```
